128 devices in a mesh: ctx: 8 (over y_lo, z), comp: 8 (over y_hi, x), grp: 2 (over core).
Axes of the slice: x: 4, y: 4 (y_hi: 2, y_lo: 2; y = y_hi * 2 + y_lo), z: 4, core: 2. Of those that a mesh axis runs over, the one named last changes fastest.
Arguments:
- prompt_query: bfloat16 [2, 4096, 1024], P('grp', 'ctx', 'comp'), may hold values from -64 to 64
- prompt_cache: bfloat16 [2, 4096, 256], P('grp', 'ctx'), may hold values from -6 to 6
- prompt_cotangent: bfloat16 [2, 4096, 1024], P('grp', 'ctx', 'comp'), may hold values from -3 to 3
- reply_query: bfloat16 [16384, 1024], P(('comp', 'grp'), 'ctx'), may hold values from -64 to 64
- reply_cache: bfloat16 [16384, 256], P(('comp', 'grp')), may hold values from -6 to 6
- reply_cotangent: bfloat16 [16384, 1024], P(('comp', 'grp'), 'ctx'), may hold values from -3 to 3
- reply_lengths: int32 [16, 4], P(('comp', 'grp')), may hold values from 0 to 512, as said below
- reply_owner: int32 [16, 4], P(('comp', 'grp')), may hold values from 0 to 1
Outputs:
- prompt_output: bfloat16 [2, 4096, 1024], P('grp', 'ctx', 'comp')
- prompt_query_grad: bfloat16 [2, 4096, 1024], P('grp', 'ctx', 'comp')
- prompt_cache_grad: bfloat16 [2, 4096, 256], P(None, ('ctx', 'comp', 'grp'))
- reply_output: bfloat16 [16384, 1024], P(('comp', 'grp'), 'ctx')
- reply_query_grad: bfloat16 [16384, 1024], P(('comp', 'grp'), 'ctx')
- reply_cache_grad: bfloat16 [16384, 256], P(('comp', 'grp'))
The draws below stay inside these ranges and needn't reach their ends.
Inputs may be any that keep to these rules, and one draw needn't show every extreme that they name: `reply_lengths`: each row sums to at most 1024; some row sums to exactly 1024 and holds a completion of exactly 512 tokens; zeros mark unused slots.
All inputs are finite; a program needn't handle non-finite values.
Results may differ from the reference program's by a relative error of at most 0.03.
Values may be sent and summed in bfloat16 or wider, within the bound.
No kernel may reach another device: no remote copies, remote signals or barrier semaphores. Data moves between devices by JAX's collectives and lax.ppermute only.
A program may use at most 128 MiB of HBM per device.

```python
import jax
import jax.numpy as jnp
from jax import lax

HD = 128
HQ = 8
CAP = 1024
SLOTS = 4
LMAX = 512
G = 2
P_SIZE = 4096
NDC = 16
C_ALL = 16384


def key_values(key, marker, row_count, width):
    base = jax.random.fold_in(key, marker)
    normal_part = jax.random.normal(jax.random.fold_in(base, 1), (row_count, width), jnp.float32)
    mixed = normal_part
    return jnp.clip(mixed, -6.0, 6.0)


def draw_values(key, marker, row_count, width):
    values = key_values(key, marker, row_count, width)
    column_scale = jnp.where(jnp.arange(width) < width // 2, 1.0, 0.5)
    return values * column_scale[None, :]


def drawn_queries(key, marker, keys_half, heads):
    base = jax.random.fold_in(key, marker)
    row_count = keys_half.shape[0]
    width = keys_half.shape[1] * heads
    drawn = jnp.clip(jax.random.normal(jax.random.fold_in(base, 1), (row_count, width), jnp.float32), -6.0, 6.0)
    return drawn


def draw_prompt_cache(key, part):
    values = draw_values(key, 11, G * P_SIZE, 2 * HD)
    return values.reshape(G, P_SIZE, 2 * HD).astype(jnp.bfloat16)


def draw_prompt_query(key, part):
    values = key_values(key, 11, G * P_SIZE, 2 * HD)
    queries = drawn_queries(key, 13, values[:, :HD], HQ)
    return queries.reshape(G, P_SIZE, HQ * HD).astype(jnp.bfloat16)


def draw_reply_cache(key, part):
    return draw_values(key, 17, C_ALL, 2 * HD).astype(jnp.bfloat16)


def draw_reply_query(key, part):
    values = key_values(key, 17, C_ALL, 2 * HD)
    return drawn_queries(key, 19, values[:, :HD], HQ).astype(jnp.bfloat16)


def draw_reply_lengths(key, part):
    key = jax.random.fold_in(key, 23)
    first_key, second_key, third_key = jax.random.split(key, 3)
    lengths = jax.random.randint(first_key, (NDC, SLOTS), 1, LMAX + 1)
    used = jax.random.randint(second_key, (NDC, 1), 1, SLOTS + 1)
    slot_ids = jnp.arange(SLOTS, dtype=jnp.int32)
    lengths = jnp.where(slot_ids[None, :] < used, lengths, 0)
    full_row = jax.random.randint(third_key, (), 0, NDC)
    pattern = jnp.where(slot_ids < 2, LMAX, 0)
    lengths = jnp.where(jnp.arange(NDC, dtype=jnp.int32)[:, None] == full_row, pattern[None, :], lengths)
    before = jnp.cumsum(lengths, axis=1) - lengths
    return jnp.minimum(lengths, jnp.maximum(CAP - before, 0)).astype(jnp.int32)


def plant(array, key, low, high):
    dims = array.shape
    spot = [jax.random.randint(jax.random.fold_in(key, axis), (), 0, dims[axis]) for axis in range(len(dims))]
    array = array.at[tuple(spot)].set(low)
    longest = dims.index(max(dims))
    spot[longest] = (spot[longest] + 1) % dims[longest]
    return array.at[tuple(spot)].set(high)


def block_scale(key, shape, cuts, least, top_value):
    factor_of = 1.0
    for dim, blocks in cuts:
        heights = jax.random.uniform(jax.random.fold_in(jax.random.fold_in(key, 6), dim), (blocks,), jnp.float32, least / len(cuts), top_value / len(cuts))
        factor_of = factor_of * jnp.repeat(jnp.exp(heights), shape[dim] // blocks).reshape((-1,) + (1,) * (len(shape) - 1 - dim))
    return factor_of


def bell_draw(own_key, shape, scale, limit, shards=(), kind=jnp.bfloat16):
    loudness = block_scale(own_key, shape, shards, -0.22, 0.18) if shards else 1.0
    drawn = jax.random.normal(own_key, shape, jnp.float32) * scale * loudness
    return jnp.minimum(jnp.maximum(drawn, -limit), limit).astype(kind)


def setup_inputs(seed: int = 0) -> dict:
    key_list = jax.random.split(jax.random.key(seed), 9)
    prompt_query = draw_prompt_query(jax.random.fold_in(key_list[8], 71), 0)
    prompt_cache = draw_prompt_cache(jax.random.fold_in(key_list[8], 71), 0)
    prompt_cotangent = bell_draw(key_list[2], (G, P_SIZE, HQ * HD), 0.5, 3.0, ((0, 2), (1, 8), (2, 8)))
    reply_query = draw_reply_query(jax.random.fold_in(key_list[8], 71), 0)
    reply_cache = draw_reply_cache(jax.random.fold_in(key_list[8], 71), 0)
    reply_cotangent = bell_draw(key_list[5], (C_ALL, HQ * HD), 0.5, 3.0, ((0, 16), (1, 8)))
    reply_lengths = draw_reply_lengths(jax.random.fold_in(key_list[8], 71), 0)
    reply_owner = plant(jax.random.randint(key_list[7], (NDC, SLOTS), 0, G), jax.random.fold_in(key_list[7], 1), 0, G - 1).astype(jnp.int32)
    return {"prompt_query": prompt_query, "prompt_cache": prompt_cache, "prompt_cotangent": prompt_cotangent, "reply_query": reply_query, "reply_cache": reply_cache, "reply_cotangent": reply_cotangent, "reply_lengths": reply_lengths, "reply_owner": reply_owner}


MASKED = -1e30


def head_pass(query_head, grad_head, key_rows, value_rows, allowed, usable, scaling):
    scores = jnp.dot(query_head, key_rows.T, preferred_element_type=jnp.float32) * scaling
    scores = jnp.where(allowed, scores, MASKED)
    highest = jnp.max(scores, axis=1, keepdims=True)
    log_total = highest + jnp.log(jnp.sum(jnp.exp(scores - highest), axis=1, keepdims=True))
    weights = jnp.exp(scores - log_total)
    rounded = weights.astype(jnp.bfloat16)
    result = jnp.dot(rounded, value_rows, preferred_element_type=jnp.float32)
    attended = jnp.where(usable[:, None], result, 0.0).astype(jnp.bfloat16)
    grad_used = jnp.where(usable[:, None], grad_head, jnp.zeros_like(grad_head))
    row_dot = jnp.sum(grad_used.astype(jnp.float32) * attended.astype(jnp.float32), axis=1, keepdims=True)
    weight_grad = jnp.dot(grad_used, value_rows.T, preferred_element_type=jnp.float32)
    score_grad = (weights * (weight_grad - row_dot)).astype(jnp.bfloat16)
    query_grad = (jnp.dot(score_grad, key_rows, preferred_element_type=jnp.float32) * scaling).astype(jnp.bfloat16)
    key_grad = jnp.dot(score_grad.T, query_head, preferred_element_type=jnp.float32) * scaling
    value_grad = jnp.dot(rounded.T, grad_used, preferred_element_type=jnp.float32)
    return attended, query_grad, jnp.concatenate([key_grad, value_grad], axis=1)


def join_heads(stacked):
    return jnp.transpose(stacked, (1, 0, 2)).reshape(stacked.shape[1], stacked.shape[0] * stacked.shape[2])


def packing(lengths, owners, capacity):
    bounds = jnp.cumsum(lengths).astype(jnp.int32)
    positions = jnp.arange(capacity, dtype=jnp.int32)
    slot_of = jnp.sum((positions[:, None] >= bounds[None, :]).astype(jnp.int32), axis=1).astype(jnp.int32)
    picks = slot_of[:, None] == jnp.arange(lengths.shape[0], dtype=jnp.int32)[None, :]
    owner_of = jnp.sum(jnp.where(picks, owners[None, :], 0), axis=1).astype(jnp.int32)
    usable = positions < bounds[-1]
    return positions, slot_of, owner_of, usable


def reference(prompt_query, prompt_cache, prompt_cotangent, reply_query, reply_cache, reply_cotangent, reply_lengths, reply_owner):
    scaling = HD ** -0.5
    head_ids = jnp.arange(HQ, dtype=jnp.int32)
    positions = jnp.arange(P_SIZE, dtype=jnp.int32)
    causal = positions[None, :] <= positions[:, None]
    everyone = jnp.ones((P_SIZE,), dtype=bool)

    def prompt_one(inputs):
        query_one, cache_one, grad_one = inputs

        def one_head(head):
            query_head = lax.dynamic_slice_in_dim(query_one, head * HD, HD, 1)
            grad_head = lax.dynamic_slice_in_dim(grad_one, head * HD, HD, 1)
            return head_pass(query_head, grad_head, cache_one[:, :HD], cache_one[:, HD:], causal, everyone, scaling)

        outputs, grads, terms = lax.map(one_head, head_ids)
        return join_heads(outputs), join_heads(grads), jnp.sum(terms, axis=0)

    prompt_out, prompt_dq, prompt_terms = lax.map(prompt_one, (prompt_query, prompt_cache, prompt_cotangent))

    flat_prompt = prompt_cache.reshape(G * P_SIZE, 2 * HD)
    key_owner = (jnp.arange(G * P_SIZE, dtype=jnp.int32) // P_SIZE).astype(jnp.int32)

    def reply_one(inputs):
        query_dev, cache_dev, grad_dev, lengths, owners = inputs
        places, slot_of, owner_of, usable = packing(lengths, owners, CAP)
        all_keys = jnp.concatenate([flat_prompt, cache_dev], axis=0)
        allowed = jnp.concatenate([owner_of[:, None] == key_owner[None, :], (slot_of[:, None] == slot_of[None, :]) & (places[None, :] <= places[:, None])], axis=1)

        def one_head(head):
            query_head = lax.dynamic_slice_in_dim(query_dev, head * HD, HD, 1)
            grad_head = lax.dynamic_slice_in_dim(grad_dev, head * HD, HD, 1)
            return head_pass(query_head, grad_head, all_keys[:, :HD], all_keys[:, HD:], allowed, usable, scaling)

        outputs, grads, terms = lax.map(one_head, head_ids)
        return join_heads(outputs), join_heads(grads), jnp.sum(terms, axis=0)

    reply_out, reply_dq, reply_terms = lax.map(reply_one, (reply_query.reshape(NDC, CAP, HQ * HD), reply_cache.reshape(NDC, CAP, 2 * HD), reply_cotangent.reshape(NDC, CAP, HQ * HD), reply_lengths, reply_owner))
    prompt_total = prompt_terms + jnp.sum(reply_terms[:, :G * P_SIZE], axis=0).reshape(G, P_SIZE, 2 * HD)
    reply_grad = reply_terms[:, G * P_SIZE:].reshape(C_ALL, 2 * HD)
    return (prompt_out, prompt_dq, prompt_total.astype(jnp.bfloat16), reply_out.reshape(C_ALL, HQ * HD), reply_dq.reshape(C_ALL, HQ * HD), reply_grad.astype(jnp.bfloat16))
```

```python
import functools
import jax
import jax.numpy as jnp
from jax import lax
from jax.experimental import pallas as pl
from jax.experimental.pallas import tpu as pltpu
from jax.sharding import PartitionSpec as P

ROWS = 256
CHUNK = 512
LOCAL = 256
LOG2E = 1.4426950408889634
MASKED = -1e30
F32 = jnp.float32
BF16 = jnp.bfloat16


def dot(a, b, ca, cb):
    return lax.dot_general(a, b, (((ca,), (cb,)), ((), ())), preferred_element_type=F32)


def run_block(q_t, do_t, scaling, parts, score_ref, weight_ref):
    head, rows = q_t.shape
    steep = scaling * LOG2E

    highest = jnp.full((8, rows), MASKED, F32)
    for cache, _, offset, size, first, last, mask in parts:

        def scores_of(c, highest, cache=cache, offset=offset, size=size, mask=mask):
            at = pl.multiple_of(c * size, size)
            scores = dot(cache[pl.ds(at, size), :head], q_t, 1, 0)
            if mask is not None:
                scores = mask(scores, at)
            score_ref[pl.ds(offset + at, size), :] = scores
            return jnp.maximum(highest, jnp.max(scores.reshape(size // 8, 8, rows), axis=0))

        highest = lax.fori_loop(first, last, scores_of, highest)
    highest = jnp.max(highest, axis=0, keepdims=True) * steep

    carry = (jnp.zeros((8, rows), F32), jnp.zeros((head, rows), F32))
    for cache, _, offset, size, first, last, _ in parts:

        def weights_of(c, carry, cache=cache, offset=offset, size=size):
            total, out = carry
            at = pl.multiple_of(c * size, size)
            weights = jnp.exp2(score_ref[pl.ds(offset + at, size), :] * steep - highest)
            total = total + jnp.sum(weights.reshape(size // 8, 8, rows), axis=0)
            rounded = weights.astype(BF16)
            weight_ref[pl.ds(offset + at, size), :] = rounded
            out = out + dot(cache[pl.ds(at, size), head:], rounded, 0, 0)
            return total, out

        carry = lax.fori_loop(first, last, weights_of, carry)
    total, out = carry
    inverse = 1.0 / jnp.sum(total, axis=0, keepdims=True)
    out = (out * inverse).astype(BF16)
    row_dot = jnp.sum(out.astype(F32) * do_t.astype(F32), axis=0, keepdims=True)
    q_scaled = (q_t.astype(F32) * (inverse * scaling)).astype(BF16)
    do_scaled = (do_t.astype(F32) * inverse).astype(BF16)

    query_grad = jnp.zeros((head, rows), F32)
    for cache, grad, offset, size, first, last, _ in parts:

        def grads_of(c, query_grad, cache=cache, grad=grad, offset=offset, size=size):
            at = pl.multiple_of(c * size, size)
            rounded = weight_ref[pl.ds(offset + at, size), :]
            weight_grad = dot(cache[pl.ds(at, size), head:], do_t, 1, 0)
            score_grad = (rounded.astype(F32) * (weight_grad - row_dot)).astype(BF16)
            grad[pl.ds(at, size), :head] += dot(score_grad, q_scaled, 1, 1)
            grad[pl.ds(at, size), head:] += dot(rounded, do_scaled, 1, 1)
            return query_grad + dot(cache[pl.ds(at, size), :head], score_grad, 0, 0)

        query_grad = lax.fori_loop(first, last, grads_of, query_grad)
    return out, (query_grad * (inverse * scaling)).astype(BF16)


def prompt_kernel(scaling, place_ref, q_ref, do_ref, cache_ref, carried_ref, arrived_ref, out_ref, dq_ref, sum_ref, grad, score_ref, weight_ref):
    length, rows_here = cache_ref.shape[0], q_ref.shape[0]
    shards = length // rows_here
    me = place_ref[0]
    grad[...] = carried_ref[...].astype(F32) + arrived_ref[...].astype(F32)

    def block(b, unused):
        here = pl.multiple_of(b * ROWS, ROWS)
        q_t = q_ref[pl.ds(here, ROWS), :].astype(F32).T.astype(BF16)
        do_t = do_ref[pl.ds(here, ROWS), :].astype(F32).T.astype(BF16)

        def causal(scores, at):
            keys = at + lax.broadcasted_iota(jnp.int32, scores.shape, 0)
            rows = here + lax.broadcasted_iota(jnp.int32, scores.shape, 1)
            return jnp.where(keys <= rows, scores, MASKED)

        whole = rows_here // CHUNK
        parts = [
            (cache_ref, grad, 0, ROWS, 0, b + 1, causal),
            (cache_ref, grad, 0, CHUNK, whole, whole * (me + 1), None),
        ]
        out, query_grad = run_block(q_t, do_t, scaling, parts, score_ref, weight_ref)
        out_ref[pl.ds(here, ROWS), :] = out.astype(F32).T.astype(BF16)
        dq_ref[pl.ds(here, ROWS), :] = query_grad.astype(F32).T.astype(BF16)
        return unused

    lax.fori_loop(0, q_ref.shape[0] // ROWS, block, 0)
    for k in range(shards):
        at = pl.multiple_of(lax.rem(me + (shards - k), shards) * rows_here, rows_here)
        sum_ref[pl.ds(at, rows_here), :] = grad[k * rows_here : (k + 1) * rows_here, :].astype(BF16)


def prompt_pass(place, q, do, cache, carried, arrived, scaling):
    rows, head = q.shape
    length = cache.shape[0]
    return pl.pallas_call(
        functools.partial(prompt_kernel, scaling),
        out_shape=[
            jax.ShapeDtypeStruct((rows, head), BF16),
            jax.ShapeDtypeStruct((rows, head), BF16),
            jax.ShapeDtypeStruct((length, 2 * head), BF16),
        ],
        in_specs=[pl.BlockSpec(memory_space=pltpu.SMEM)] + [pl.BlockSpec(memory_space=pltpu.VMEM)] * 5,
        out_specs=[pl.BlockSpec(memory_space=pltpu.VMEM)] * 3,
        scratch_shapes=[
            pltpu.VMEM((length, 2 * head), F32),
            pltpu.VMEM((length, ROWS), F32),
            pltpu.VMEM((length, ROWS), BF16),
        ],
        compiler_params=pltpu.CompilerParams(vmem_limit_bytes=48 * 1024 * 1024),
        name="prompt_pass",
    )(place, q, do, cache, carried, arrived)


def reply_kernel(scaling, which_ref, lengths_ref, owners_ref, q_ref, do_ref, cache_ref, own_ref, *refs):
    out_ref, dq_ref, sum_ref, own_sum_ref, q_t_ref, do_t_ref, out_t, dq_t, grad, own_grad, score_ref, weight_ref = refs[-12:]
    before = refs[:-12]
    capacity, head = q_ref.shape
    length = cache_ref.shape[0]
    slots = lengths_ref.shape[0]
    starts, ranks, counts = [], [], []
    at, rank = jnp.int32(0), jnp.int32(0)
    for s in range(slots):
        count = jnp.where(owners_ref[s] == which_ref[0], lengths_ref[s], 0)
        starts.append(at)
        ranks.append(rank)
        counts.append(count)
        at = at + lengths_ref[s]
        rank = rank + count
    blocks = (rank + ROWS - 1) // ROWS

    q_t_ref[...] = q_ref[...].astype(F32).T.astype(BF16)
    do_t_ref[...] = do_ref[...].astype(F32).T.astype(BF16)
    out_t[...] = jnp.zeros_like(out_t)
    dq_t[...] = jnp.zeros_like(dq_t)
    grad[...] = jnp.zeros_like(grad)
    if before:
        own_grad[...] = before[2][...]
    else:
        own_grad[...] = jnp.zeros_like(own_grad)

    def block(b, unused):
        first_rank = b * ROWS
        place_of = first_rank + lax.broadcasted_iota(jnp.int32, (1, ROWS), 1)
        place = jnp.full((1, ROWS), -1, jnp.int32)
        start = jnp.zeros((1, ROWS), jnp.int32)
        low, high = jnp.int32(capacity), jnp.int32(0)
        for s in range(slots):
            inside = (place_of >= ranks[s]) & (place_of < ranks[s] + counts[s])
            place = jnp.where(inside, place_of + (starts[s] - ranks[s]), place)
            start = jnp.where(inside, starts[s], start)
            begin = jnp.maximum(ranks[s], first_rank)
            end = jnp.minimum(ranks[s] + counts[s], first_rank + ROWS)
            some = begin < end
            low = jnp.where(some, jnp.minimum(low, starts[s]), low)
            high = jnp.where(some, jnp.maximum(high, end + (starts[s] - ranks[s])), high)
        picks = jnp.where(
            lax.broadcasted_iota(jnp.int32, (capacity, ROWS), 0) == place, 1.0, 0.0
        ).astype(BF16)
        q_t = dot(q_t_ref[...], picks, 1, 0).astype(BF16)
        do_t = dot(do_t_ref[...], picks, 1, 0).astype(BF16)

        def packed(scores, at):
            keys = at + lax.broadcasted_iota(jnp.int32, scores.shape, 0)
            return jnp.where((keys >= start) & (keys <= place), scores, MASKED)

        parts = [
            (cache_ref, grad, 0, CHUNK, 0, length // CHUNK, None),
            (own_ref, own_grad, length, LOCAL, low // LOCAL, (high + LOCAL - 1) // LOCAL, packed),
        ]
        out, query_grad = run_block(q_t, do_t, scaling, parts, score_ref, weight_ref)
        out_t[...] += dot(out, picks, 1, 1)
        dq_t[...] += dot(query_grad, picks, 1, 1)
        return unused

    lax.fori_loop(0, blocks, block, 0)
    out = out_t[...].T
    query_grad = dq_t[...].T
    if before:
        out = out + before[0][...].astype(F32)
        query_grad = query_grad + before[1][...].astype(F32)
    out_ref[...] = out.astype(BF16)
    dq_ref[...] = query_grad.astype(BF16)
    sum_ref[...] = grad[...].astype(BF16)
    own_sum_ref[...] = own_grad[...].astype(own_sum_ref.dtype)


def reply_pass(which, lengths, owners, q, do, cache, own, before, own_type, scaling):
    capacity, head = q.shape
    length = cache.shape[0]
    return pl.pallas_call(
        functools.partial(reply_kernel, scaling),
        out_shape=[
            jax.ShapeDtypeStruct((capacity, head), BF16),
            jax.ShapeDtypeStruct((capacity, head), BF16),
            jax.ShapeDtypeStruct((length, 2 * head), BF16),
            jax.ShapeDtypeStruct((capacity, 2 * head), own_type),
        ],
        in_specs=[pl.BlockSpec(memory_space=pltpu.SMEM)] * 3
        + [pl.BlockSpec(memory_space=pltpu.VMEM)] * (4 + len(before)),
        out_specs=[pl.BlockSpec(memory_space=pltpu.VMEM)] * 4,
        scratch_shapes=[
            pltpu.VMEM((head, capacity), BF16),
            pltpu.VMEM((head, capacity), BF16),
            pltpu.VMEM((head, capacity), F32),
            pltpu.VMEM((head, capacity), F32),
            pltpu.VMEM((length, 2 * head), F32),
            pltpu.VMEM((capacity, 2 * head), F32),
            pltpu.VMEM((length + capacity, ROWS), F32),
            pltpu.VMEM((length + capacity, ROWS), BF16),
        ],
        compiler_params=pltpu.CompilerParams(vmem_limit_bytes=48 * 1024 * 1024),
        name="reply_pass",
    )(which, lengths, owners, q, do, cache, own, *before)


def per_device(
    prompt_query,
    prompt_cache,
    prompt_cotangent,
    reply_query,
    reply_cache,
    reply_cotangent,
    reply_lengths,
    reply_owner,
):
    width = prompt_cache.shape[2]
    scaling = (width // 2) ** (-0.5)
    row_count = prompt_query.shape[1]
    capacity = reply_query.shape[0]
    ctx_count, comp_count, group_count = (lax.axis_size(name) for name in ("ctx", "comp", "grp"))
    place = lax.axis_index("ctx").astype(jnp.int32).reshape(1)
    group = lax.axis_index("grp").astype(jnp.int32).reshape(1)
    swap = [(0, 1), (1, 0)]

    with jax.named_scope("gather_keys"):
        own = prompt_cache[0]
        shards = [own] + [
            lax.ppermute(own, "ctx", [(i, (i + k) % ctx_count) for i in range(ctx_count)])
            for k in range(1, ctx_count)
        ]
        mine = jnp.concatenate(shards, axis=0)
        other = lax.ppermute(mine, "grp", swap)

    lengths, owners = reply_lengths[0], reply_owner[0]
    with jax.named_scope("reply_other"):
        out1, dq1, sum1, own1 = reply_pass(
            1 - group, lengths, owners, reply_query, reply_cotangent, other, reply_cache, [], F32, scaling
        )
    arrived = lax.ppermute(sum1, "grp", swap)
    with jax.named_scope("reply_own"):
        reply_out, reply_dq, sum2, own2 = reply_pass(
            group, lengths, owners, reply_query, reply_cotangent, mine, reply_cache, [out1, dq1, own1], BF16, scaling
        )
    with jax.named_scope("prompt_rows"):
        prompt_out, prompt_dq, total = prompt_pass(
            place, prompt_query[0], prompt_cotangent[0], mine, sum2, arrived, scaling
        )

    with jax.named_scope("reply_cache_sum"):
        terms = lax.all_to_all(own2.reshape(ctx_count, -1, width), "ctx", 0, 0, tiled=True)
        part = jnp.sum(terms.astype(F32), axis=0).astype(BF16)
        reply_grad = lax.all_to_all(
            jnp.broadcast_to(part[None], (ctx_count,) + part.shape), "ctx", 0, 0, tiled=True
        ).reshape(capacity, width)

    with jax.named_scope("prompt_cache_sum"):
        count = ctx_count * comp_count
        terms = lax.all_to_all(total.reshape(count, -1, width), ("ctx", "comp"), 0, 0, tiled=True)
        part = jnp.sum(terms.astype(F32), axis=0).astype(BF16)
        prompt_grad = lax.all_to_all(part.reshape(group_count, -1, width), "grp", 0, 0, tiled=True)
    return (
        prompt_out[None],
        prompt_dq[None],
        prompt_grad,
        reply_out,
        reply_dq,
        reply_grad,
    )


def solution(mesh):
    return jax.shard_map(
        per_device,
        mesh=mesh,
        in_specs=(
            P("grp", "ctx", "comp"),
            P("grp", "ctx", None),
            P("grp", "ctx", "comp"),
            P(("comp", "grp"), "ctx"),
            P(("comp", "grp"), None),
            P(("comp", "grp"), "ctx"),
            P(("comp", "grp"), None),
            P(("comp", "grp"), None),
        ),
        out_specs=(
            P("grp", "ctx", "comp"),
            P("grp", "ctx", "comp"),
            P(None, ("ctx", "comp", "grp"), None),
            P(("comp", "grp"), "ctx"),
            P(("comp", "grp"), "ctx"),
            P(("comp", "grp"), None),
        ),
        check_vma=False,
    )
```

```python
import functools
import jax
import jax.numpy as jnp
from jax import lax
from jax.experimental import pallas as pl
from jax.experimental.pallas import tpu as pltpu
from jax.sharding import PartitionSpec as P

ROWS = 256
CHUNK = 512
LOG2E = 1.4426950408889634
MASKED = -1e30
F32 = jnp.float32
BF16 = jnp.bfloat16


def dot(a, b, ca, cb):
    return lax.dot_general(a, b, (((ca,), (cb,)), ((), ())), preferred_element_type=F32)


def turned(x):
    return x.astype(F32).T.astype(BF16)


def run_block(q_t, do_t, scaling, pieces, extra, score_ref, weight_ref, slope_ref=None):
    head, rows = q_t.shape
    steep = scaling * LOG2E

    def each(step, carry):
        for piece in pieces:
            carry = step(piece, carry)
        if extra is not None:
            carry = lax.fori_loop(1, extra[0], lambda w, c: step(extra[1](w), c), carry)
        return carry

    def scores_of(piece, highest):
        cache, at, _, _, row, size, mask = piece
        scores = dot(cache[pl.ds(at, size), :head], q_t, 1, 0)
        if mask is not None:
            scores = mask(scores)
        score_ref[pl.ds(row, size), :] = scores
        return jnp.maximum(highest, jnp.max(scores.reshape(size // 8, 8, rows), axis=0))

    highest = each(scores_of, jnp.full((8, rows), MASKED, F32))
    highest = jnp.max(highest, axis=0, keepdims=True) * steep

    def weights_of(piece, carry):
        cache, at, _, _, row, size, _ = piece
        total, out = carry
        weights = jnp.exp2(score_ref[pl.ds(row, size), :] * steep - highest)
        total = total + jnp.sum(weights.reshape(size // 8, 8, rows), axis=0)
        rounded = weights.astype(BF16)
        weight_ref[pl.ds(row, size), :] = rounded
        if slope_ref is not None:
            slope_ref[pl.ds(row, size), :] = dot(cache[pl.ds(at, size), head:], do_t, 1, 0)
        return total, out + dot(cache[pl.ds(at, size), head:], rounded, 0, 0)

    total, out = each(weights_of, (jnp.zeros((8, rows), F32), jnp.zeros((head, rows), F32)))
    inverse = 1.0 / jnp.sum(total, axis=0, keepdims=True)
    out = (out * inverse).astype(BF16)
    row_dot = jnp.sum(out.astype(F32) * do_t.astype(F32), axis=0, keepdims=True)
    q_scaled = turned(q_t.astype(F32) * (inverse * scaling))
    do_scaled = turned(do_t.astype(F32) * inverse)

    def grads_of(piece, query_grad):
        cache, at, grad, to, row, size, _ = piece
        rounded = weight_ref[pl.ds(row, size), :]
        if slope_ref is not None:
            weight_grad = slope_ref[pl.ds(row, size), :]
        else:
            weight_grad = dot(cache[pl.ds(at, size), head:], do_t, 1, 0)
        score_grad = (rounded.astype(F32) * (weight_grad - row_dot)).astype(BF16)
        grad[pl.ds(to, size), :head] += dot(score_grad, q_scaled, 1, 0)
        grad[pl.ds(to, size), head:] += dot(rounded, do_scaled, 1, 0)
        return query_grad + dot(cache[pl.ds(at, size), :head], score_grad, 0, 0)

    query_grad = each(grads_of, jnp.zeros((head, rows), F32))
    return out, (query_grad * (inverse * scaling)).astype(BF16)


def leave_in_order(me, inner, rows_here, grad, sum_ref):
    for k in range(grad.shape[0] // rows_here):
        outer = lax.div(me, inner) if k < inner else 1 - lax.div(me, inner)
        place = outer * inner + lax.rem(lax.rem(me, inner) + (2 * inner - k), inner)
        at = pl.multiple_of(place * rows_here, rows_here)
        sum_ref[pl.ds(at, rows_here), :] = grad[k * rows_here : (k + 1) * rows_here, :].astype(BF16)


def prompt_kernel(scaling, inner, place_ref, q_ref, do_ref, *refs):
    caches, (carried_ref, out_ref, dq_ref, sum_ref, grad, score_ref, weight_ref) = refs[:-7], refs[-7:]
    length, rows_here = grad.shape[0], q_ref.shape[0]
    half = length // 2
    me_outer, me_inner = lax.div(place_ref[0], inner), lax.rem(place_ref[0], inner)
    grad[...] = carried_ref[...].astype(F32)

    def block(b, unused):
        here = pl.multiple_of(b * ROWS, ROWS)

        def causal(scores):
            keys = lax.broadcasted_iota(jnp.int32, scores.shape, 0)
            rows = here + lax.broadcasted_iota(jnp.int32, scores.shape, 1)
            return jnp.where(keys <= rows, scores, MASKED)

        def earlier(at, scores):
            keys = at + lax.broadcasted_iota(jnp.int32, scores.shape, 0)
            limit = rows_here * (me_inner + 1) if at < half else length * me_outer
            return jnp.where(keys < limit, scores, MASKED)

        pieces, at = [], 0
        for cache_ref in caches:
            begin = 0
            while begin < cache_ref.shape[0]:
                size = rows_here if at == 0 else min(CHUNK, cache_ref.shape[0] - begin)
                mask = causal if at == 0 else functools.partial(earlier, at)
                pieces.append((cache_ref, begin, grad, at, at, size, mask))
                at, begin = at + size, begin + size
        out, query_grad = run_block(
            turned(q_ref[pl.ds(here, ROWS), :]), turned(do_ref[pl.ds(here, ROWS), :]), scaling, pieces, None, score_ref, weight_ref
        )
        out_ref[pl.ds(here, ROWS), :] = turned(out)
        dq_ref[pl.ds(here, ROWS), :] = turned(query_grad)
        return unused

    lax.fori_loop(0, rows_here // ROWS, block, 0)
    leave_in_order(place_ref[0], inner, rows_here, grad, sum_ref)


def prompt_pass(place, inner, q, do, caches, carried, scaling):
    rows, head = q.shape
    length = carried.shape[0]
    return pl.pallas_call(
        functools.partial(prompt_kernel, scaling, inner),
        out_shape=[
            jax.ShapeDtypeStruct((rows, head), BF16),
            jax.ShapeDtypeStruct((rows, head), BF16),
            jax.ShapeDtypeStruct((length, 2 * head), BF16),
        ],
        in_specs=[pl.BlockSpec(memory_space=pltpu.SMEM)] + [pl.BlockSpec(memory_space=pltpu.VMEM)] * (3 + len(caches)),
        out_specs=[pl.BlockSpec(memory_space=pltpu.VMEM)] * 3,
        scratch_shapes=[
            pltpu.VMEM((length, 2 * head), F32),
            pltpu.VMEM((length, ROWS), F32),
            pltpu.VMEM((length, ROWS), BF16),
        ],
        compiler_params=pltpu.CompilerParams(vmem_limit_bytes=24 * 1024 * 1024),
        cost_estimate=pl.CostEstimate(flops=24 * rows * length * head, bytes_accessed=8 * length * head, transcendentals=0),
        name="prompt_pass",
    )(place, q, do, *caches, carried)


def reply_kernel(
    scaling, inner, other_count, scalars_ref, lengths_ref, owners_ref, q_ref, do_ref, own_ref, *refs
):
    (
        out_ref, dq_ref, other_sum_ref, mine_sum_ref, own_keep_ref, own_send_ref,
        picks_ref, q_t_ref, do_t_ref, results, grad, own_grad, score_ref, weight_ref, slope_ref,
    ) = refs[-15:]
    caches = refs[:-15]
    others, mines = caches[:other_count], caches[other_count:]
    capacity, head = q_ref.shape
    length = grad.shape[0]
    slots = lengths_ref.shape[0]
    window = capacity // 2

    starts, ranks, counts = [], [], []
    total = jnp.int32(0)
    edges = [total]
    for of_mine in (False, True):
        place_now = jnp.int32(0)
        for s in range(slots):
            taken = (owners_ref[s] == scalars_ref[1]) == of_mine
            count = jnp.where(taken, lengths_ref[s], 0)
            starts.append(place_now)
            ranks.append(total)
            counts.append(count)
            place_now = place_now + lengths_ref[s]
            total = total + count
        total = (total + ROWS - 1) // ROWS * ROWS
        edges.append(total)

    def located(rank_of):
        place = jnp.full(rank_of.shape, -1, jnp.int32)
        start = jnp.zeros(rank_of.shape, jnp.int32)
        for s in range(2 * slots):
            inside = (rank_of >= ranks[s]) & (rank_of < ranks[s] + counts[s])
            place = jnp.where(inside, rank_of + (starts[s] - ranks[s]), place)
            start = jnp.where(inside, starts[s], start)
        return place, start

    spread = q_t_ref.shape[1]
    place_all, _ = located(lax.broadcasted_iota(jnp.int32, (1, spread), 1))
    picks_ref[...] = jnp.where(
        lax.broadcasted_iota(jnp.int32, (capacity, spread), 0) == place_all, 1.0, 0.0
    ).astype(BF16)
    q_t_ref[...] = dot(turned(q_ref[...]), picks_ref[...], 1, 0).astype(BF16)
    do_t_ref[...] = dot(turned(do_ref[...]), picks_ref[...], 1, 0).astype(BF16)
    results[...] = jnp.zeros_like(results)
    own_grad[...] = jnp.zeros_like(own_grad)

    for parts, sum_ref, edge in ((others, other_sum_ref, 0), (mines, mine_sum_ref, 1)):
        grad[...] = jnp.zeros_like(grad)

        def block(b, unused):
            first_rank = pl.multiple_of(b * ROWS, ROWS)
            here = pl.ds(first_rank, ROWS)
            low, high = jnp.int32(capacity), jnp.int32(0)
            for s in range(2 * slots):
                begin = jnp.maximum(ranks[s], first_rank)
                end = jnp.minimum(ranks[s] + counts[s], first_rank + ROWS)
                some = begin < end
                low = jnp.where(some, jnp.minimum(low, starts[s]), low)
                high = jnp.where(some, jnp.maximum(high, end + (starts[s] - ranks[s])), high)
            low = (low // 32) * 32
            place, start = located(first_rank + lax.broadcasted_iota(jnp.int32, (1, ROWS), 1))

            def own_piece(w):
                begin = low + w * window
                at = pl.multiple_of(jnp.minimum(begin, capacity - window), 32)

                def packed(scores):
                    keys = at + lax.broadcasted_iota(jnp.int32, scores.shape, 0)
                    return jnp.where((keys >= jnp.maximum(start, begin)) & (keys <= place), scores, MASKED)

                return own_ref, at, own_grad, at, length + w * window, window, packed

            pieces, at = [], 0
            for cache_ref in parts:
                for begin in range(0, cache_ref.shape[0], CHUNK):
                    size = min(CHUNK, cache_ref.shape[0] - begin)
                    pieces.append((cache_ref, begin, grad, at, at, size, None))
                    at += size
            pieces.append(own_piece(0))
            extra = ((high - low + window - 1) // window, own_piece)
            out, query_grad = run_block(
                q_t_ref[:, here], do_t_ref[:, here], scaling, pieces, extra, score_ref, weight_ref, slope_ref
            )
            results[here, :head] = turned(out)
            results[here, head:] = turned(query_grad)
            return unused

        lax.fori_loop(edges[edge] // ROWS, edges[edge + 1] // ROWS, block, 0)
        if edge == 0:
            leave_in_order(scalars_ref[0], inner, length // (2 * inner), grad, sum_ref)
        else:
            sum_ref[...] = grad[...].astype(BF16)

    placed = dot(picks_ref[...], results[...], 1, 0).astype(BF16)
    out_ref[...] = placed[:, :head]
    dq_ref[...] = placed[:, head:]
    share = capacity // (2 * inner)
    me_outer, me_inner = lax.div(scalars_ref[0], inner), lax.rem(scalars_ref[0], inner)
    for k in range(inner):
        there = lax.rem(me_inner + k, inner)
        for outer, ref in ((me_outer, own_keep_ref), (1 - me_outer, own_send_ref)):
            at = pl.multiple_of((outer * inner + there) * share, share)
            ref[k * share : (k + 1) * share, :] = own_grad[pl.ds(at, share), :].astype(BF16)


def reply_pass(scalars, inner, lengths, owners, q, do, own, others, mines, scaling):
    capacity, head = q.shape
    length = sum(part.shape[0] for part in mines)
    spread = capacity + ROWS
    return pl.pallas_call(
        functools.partial(reply_kernel, scaling, inner, len(others)),
        out_shape=[
            jax.ShapeDtypeStruct((capacity, head), BF16),
            jax.ShapeDtypeStruct((capacity, head), BF16),
            jax.ShapeDtypeStruct((length, 2 * head), BF16),
            jax.ShapeDtypeStruct((length, 2 * head), BF16),
            jax.ShapeDtypeStruct((capacity // 2, 2 * head), BF16),
            jax.ShapeDtypeStruct((capacity // 2, 2 * head), BF16),
        ],
        in_specs=[pl.BlockSpec(memory_space=pltpu.SMEM)] * 3 + [pl.BlockSpec(memory_space=pltpu.VMEM)] * (3 + len(others) + len(mines)),
        out_specs=[pl.BlockSpec(memory_space=pltpu.VMEM)] * 6,
        scratch_shapes=[
            pltpu.VMEM((capacity, spread), BF16),
            pltpu.VMEM((head, spread), BF16),
            pltpu.VMEM((head, spread), BF16),
            pltpu.VMEM((spread, 2 * head), BF16),
            pltpu.VMEM((length, 2 * head), F32),
            pltpu.VMEM((capacity, 2 * head), F32),
            pltpu.VMEM((length + capacity, ROWS), F32),
            pltpu.VMEM((length + capacity, ROWS), BF16),
            pltpu.VMEM((length + capacity, ROWS), F32),
        ],
        compiler_params=pltpu.CompilerParams(vmem_limit_bytes=36 * 1024 * 1024),
        cost_estimate=pl.CostEstimate(flops=24 * capacity * length * head, bytes_accessed=16 * length * head, transcendentals=0),
        name="reply_pass",
    )(scalars, lengths, owners, q, do, own, *others, *mines)


def place_kernel(inner, first, place_ref, *refs):
    out_ref, halves = refs[-1], (refs[:first], refs[first:-1])
    share = out_ref.shape[0] // (2 * inner)
    me_outer, me_inner = lax.div(place_ref[0], inner), lax.rem(place_ref[0], inner)
    for outer, pieces in zip((me_outer, 1 - me_outer), halves):
        at = 0
        for ref in pieces:
            for begin in range(0, ref.shape[0], share):
                there = outer * inner + lax.rem(me_inner + (inner - at), inner)
                out_ref[pl.ds(pl.multiple_of(there * share, share), share), :] = ref[begin : begin + share, :]
                at += 1


def placed_in_order(place, inner, mine, other):
    rows = sum(x.shape[0] for x in mine)
    operands = [*mine, *other]
    return pl.pallas_call(
        functools.partial(place_kernel, inner, len(mine)),
        out_shape=jax.ShapeDtypeStruct((2 * rows, mine[0].shape[1]), BF16),
        in_specs=[pl.BlockSpec(memory_space=pltpu.SMEM)] + [pl.BlockSpec(memory_space=pltpu.VMEM)] * len(operands),
        out_specs=pl.BlockSpec(memory_space=pltpu.VMEM),
        compiler_params=pltpu.CompilerParams(vmem_limit_bytes=8 * 1024 * 1024),
        name="placed_in_order",
    )(place, *operands)


def join_kernel(total_ref, arrived_ref, keep_ref, came_ref, shares_ref, *pieces):
    shares_ref[...] = (total_ref[...].astype(F32) + arrived_ref[...].astype(F32)).astype(BF16)
    rows = pieces[0].shape[0]
    for k, ref in enumerate(pieces):
        at = slice(k * rows, (k + 1) * rows)
        ref[...] = (keep_ref[at, :].astype(F32) + came_ref[at, :].astype(F32)).astype(BF16)


def join(total, arrived, keep, came, count):
    rows, width = keep.shape
    return pl.pallas_call(
        join_kernel,
        out_shape=[jax.ShapeDtypeStruct(total.shape, BF16)]
        + [jax.ShapeDtypeStruct((rows // count, width), BF16)] * count,
        in_specs=[pl.BlockSpec(memory_space=pltpu.VMEM)] * 4,
        out_specs=[pl.BlockSpec(memory_space=pltpu.VMEM)] * (1 + count),
        compiler_params=pltpu.CompilerParams(vmem_limit_bytes=16 * 1024 * 1024),
        name="join_sums",
    )(total, arrived, keep, came)


def per_device(
    prompt_query,
    prompt_cache,
    prompt_cotangent,
    reply_query,
    reply_cache,
    reply_cotangent,
    reply_lengths,
    reply_owner,
):
    width = prompt_cache.shape[2]
    scaling = (width // 2) ** (-0.5)
    capacity = reply_query.shape[0]
    ctx_count, comp_count, group_count = (lax.axis_size(name) for name in ("ctx", "comp", "grp"))
    inner, comp_inner = ctx_count // 2, comp_count // 2
    place = lax.axis_index("ctx").astype(jnp.int32).reshape(1)
    group = lax.axis_index("grp").astype(jnp.int32).reshape(1)

    def swap(x):
        return lax.ppermute(x, "grp", [(0, 1), (1, 0)])

    def along_z(x, k):
        pairs = [(i, i // inner * inner + (i + k) % inner) for i in range(ctx_count)]
        return lax.ppermute(x, "ctx", pairs)

    def outer_swap(x):
        return lax.ppermute(x, "ctx", [(i, (i + inner) % ctx_count) for i in range(ctx_count)])

    def along_y(x, k):
        pairs = []
        for ctx in range(ctx_count):
            for comp in range(comp_count):
                y = (2 * (comp // comp_inner) + ctx // inner + k) % 4
                to_ctx = y % 2 * inner + ctx % inner
                to_comp = y // 2 * comp_inner + comp % comp_inner
                pairs.append((ctx * comp_count + comp, to_ctx * comp_count + to_comp))
        return lax.ppermute(x, ("ctx", "comp"), pairs)

    with jax.named_scope("gather_keys"):
        own = prompt_cache[0]
        next_1, next_3, next_2 = along_z(own, 1), along_z(own, inner - 1), along_z(own, 2)
        y_0 = along_y(own, 1)
        y_1, y_3 = along_y(next_1, 1), along_y(next_3, -1)
        half = own.shape[0] // 2
        y_2a, y_2b = along_y(next_2[:half], 1), along_y(next_2[half:], -1)
        mines = [own, next_1, next_2, next_3, y_0, y_1, y_2a, y_2b, y_3]
        others = [swap(jnp.concatenate(part, axis=0)) for part in (mines[:inner], mines[inner:])]

    with jax.named_scope("reply_rows"):
        reply_out, reply_dq, other_sum, mine_sum, own_keep, own_send = reply_pass(
            jnp.concatenate([place, group]), inner, reply_lengths[0], reply_owner[0], reply_query, reply_cotangent, reply_cache,
            others, mines, scaling,
        )
    arrived = swap(other_sum)
    with jax.named_scope("prompt_rows"):
        prompt_out, prompt_dq, total = prompt_pass(
            place, inner, prompt_query[0], prompt_cotangent[0], mines, mine_sum, scaling
        )

    with jax.named_scope("prompt_cache_sum"):
        count = ctx_count * comp_count
        shares, *pieces = join(total, arrived, own_keep, outer_swap(own_send), inner)
        terms = lax.all_to_all(shares.reshape(count, -1, width), ("ctx", "comp"), 0, 0, tiled=True)
    with jax.named_scope("reply_cache_sum"):
        part = pieces[0].astype(F32)
        for k in range(1, inner):
            part = part + along_z(pieces[k], k).astype(F32)
        part = part.astype(BF16)
        mine_half = jnp.concatenate([part] + [along_z(part, k) for k in range(1, inner)], axis=0)
        reply_grad = placed_in_order(place, inner, [mine_half], [outer_swap(mine_half)])
    with jax.named_scope("prompt_cache_halves"):
        summed = jnp.sum(terms.astype(F32), axis=0).astype(BF16)
        rows = summed.shape[0] // group_count
        first, second = summed[:rows], summed[rows:]
        is_first = group[0] == 0
        kept = jnp.where(is_first, first, second)
        came = swap(jnp.where(is_first, second, first))
        prompt_grad = jnp.where(is_first, jnp.stack([kept, came]), jnp.stack([came, kept]))
    return (
        prompt_out[None],
        prompt_dq[None],
        prompt_grad,
        reply_out,
        reply_dq,
        reply_grad,
    )


def solution(mesh):
    return jax.shard_map(
        per_device,
        mesh=mesh,
        in_specs=(
            P("grp", "ctx", "comp"),
            P("grp", "ctx", None),
            P("grp", "ctx", "comp"),
            P(("comp", "grp"), "ctx"),
            P(("comp", "grp"), None),
            P(("comp", "grp"), "ctx"),
            P(("comp", "grp"), None),
            P(("comp", "grp"), None),
        ),
        out_specs=(
            P("grp", "ctx", "comp"),
            P("grp", "ctx", "comp"),
            P(None, ("ctx", "comp", "grp"), None),
            P(("comp", "grp"), "ctx"),
            P(("comp", "grp"), "ctx"),
            P(("comp", "grp"), None),
        ),
        check_vma=False,
    )
```

```python
import functools
import jax
import jax.numpy as jnp
from jax import lax
from jax.experimental import pallas as pl
from jax.experimental.pallas import tpu as pltpu
from jax.sharding import PartitionSpec as P

ROWS = 256
PROMPT_ROWS = 512
CHUNK = 512
LOG2E = 1.4426950408889634
MASKED = -1e30
F32 = jnp.float32
BF16 = jnp.bfloat16


def dot(a, b, ca, cb):
    return lax.dot_general(a, b, (((ca,), (cb,)), ((), ())), preferred_element_type=F32)


def turned(x):
    return x.astype(F32).T.astype(BF16)


def run_block(q_t, do_t, scaling, pieces, extra, score_ref, weight_ref, slope_ref=None):
    head, rows = q_t.shape
    steep = scaling * LOG2E

    def each(step, carry):
        for piece in pieces:
            carry = step(piece, carry)
        if extra is not None:
            carry = lax.fori_loop(1, extra[0], lambda w, c: step(extra[1](w), c), carry)
        return carry

    def scores_of(piece, highest):
        cache, at, _, _, row, size, mask = piece
        scores = dot(cache[pl.ds(at, size), :head], q_t, 1, 0)
        if mask is not None:
            scores = mask(scores)
        score_ref[pl.ds(row, size), :] = scores
        return jnp.maximum(highest, jnp.max(scores.reshape(size // 8, 8, rows), axis=0))

    highest = each(scores_of, jnp.full((8, rows), MASKED, F32))
    highest = jnp.max(highest, axis=0, keepdims=True) * steep

    def weights_of(piece, carry):
        cache, at, _, _, row, size, _ = piece
        total, out = carry
        weights = jnp.exp2(score_ref[pl.ds(row, size), :] * steep - highest)
        total = total + jnp.sum(weights.reshape(size // 8, 8, rows), axis=0)
        rounded = weights.astype(BF16)
        weight_ref[pl.ds(row, size), :] = rounded
        if slope_ref is not None:
            slope_ref[pl.ds(row, size), :] = dot(cache[pl.ds(at, size), head:], do_t, 1, 0)
        return total, out + dot(cache[pl.ds(at, size), head:], rounded, 0, 0)

    total, out = each(weights_of, (jnp.zeros((8, rows), F32), jnp.zeros((head, rows), F32)))
    inverse = 1.0 / jnp.sum(total, axis=0, keepdims=True)
    out = (out * inverse).astype(BF16)
    row_dot = jnp.sum(out.astype(F32) * do_t.astype(F32), axis=0, keepdims=True)
    q_scaled = turned(q_t.astype(F32) * (inverse * scaling))
    do_scaled = turned(do_t.astype(F32) * inverse)

    def grads_of(piece, query_grad):
        cache, at, grad, to, row, size, _ = piece
        rounded = weight_ref[pl.ds(row, size), :]
        if slope_ref is not None:
            weight_grad = slope_ref[pl.ds(row, size), :]
        else:
            weight_grad = dot(cache[pl.ds(at, size), head:], do_t, 1, 0)
        score_grad = (rounded.astype(F32) * (weight_grad - row_dot)).astype(BF16)
        grad[pl.ds(to, size), :head] += dot(score_grad, q_scaled, 1, 0)
        grad[pl.ds(to, size), head:] += dot(rounded, do_scaled, 1, 0)
        return query_grad + dot(cache[pl.ds(at, size), :head], score_grad, 0, 0)

    query_grad = each(grads_of, jnp.zeros((head, rows), F32))
    return out, (query_grad * (inverse * scaling)).astype(BF16)


def leave_in_order(me, inner, rows_here, order, grad, sum_ref):
    for i, k in enumerate(order):
        outer = lax.div(me, inner) if k < inner else 1 - lax.div(me, inner)
        place = outer * inner + lax.rem(lax.rem(me, inner) + (2 * inner - k), inner)
        at = pl.multiple_of(place * rows_here, rows_here)
        sum_ref[pl.ds(at, rows_here), :] = grad[i * rows_here : (i + 1) * rows_here, :].astype(BF16)


def prompt_kernel(scaling, inner, place_ref, q_ref, do_ref, *refs):
    caches, (carried_ref, out_ref, dq_ref, sum_ref, grad, score_ref, weight_ref) = refs[:-7], refs[-7:]
    length, rows_here = grad.shape[0], q_ref.shape[0]
    half = length // 2
    me_outer, me_inner = lax.div(place_ref[0], inner), lax.rem(place_ref[0], inner)
    grad[...] = carried_ref[...].astype(F32)

    def block(b, unused):
        here = pl.multiple_of(b * PROMPT_ROWS, PROMPT_ROWS)

        def causal(scores):
            keys = lax.broadcasted_iota(jnp.int32, scores.shape, 0)
            rows = here + lax.broadcasted_iota(jnp.int32, scores.shape, 1)
            return jnp.where(keys <= rows, scores, MASKED)

        def earlier(at, scores):
            keys = at + lax.broadcasted_iota(jnp.int32, scores.shape, 0)
            limit = rows_here * (me_inner + 1) if at < half else length * me_outer
            return jnp.where(keys < limit, scores, MASKED)

        pieces, at = [], 0
        for cache_ref in caches:
            begin = 0
            while begin < cache_ref.shape[0]:
                size = rows_here if at == 0 else min(CHUNK, cache_ref.shape[0] - begin)
                mask = causal if at == 0 else functools.partial(earlier, at)
                pieces.append((cache_ref, begin, grad, at, at, size, mask))
                at, begin = at + size, begin + size
        out, query_grad = run_block(
            turned(q_ref[pl.ds(here, PROMPT_ROWS), :]), turned(do_ref[pl.ds(here, PROMPT_ROWS), :]), scaling, pieces, None, score_ref, weight_ref
        )
        out_ref[pl.ds(here, PROMPT_ROWS), :] = turned(out)
        dq_ref[pl.ds(here, PROMPT_ROWS), :] = turned(query_grad)
        return unused

    lax.fori_loop(0, rows_here // PROMPT_ROWS, block, 0)
    leave_in_order(place_ref[0], inner, rows_here, range(2 * inner), grad, sum_ref)


def prompt_pass(place, inner, q, do, caches, carried, scaling):
    rows, head = q.shape
    length = carried.shape[0]
    return pl.pallas_call(
        functools.partial(prompt_kernel, scaling, inner),
        out_shape=[
            jax.ShapeDtypeStruct((rows, head), BF16),
            jax.ShapeDtypeStruct((rows, head), BF16),
            jax.ShapeDtypeStruct((length, 2 * head), BF16),
        ],
        in_specs=[pl.BlockSpec(memory_space=pltpu.SMEM)] + [pl.BlockSpec(memory_space=pltpu.VMEM)] * (3 + len(caches)),
        out_specs=[pl.BlockSpec(memory_space=pltpu.VMEM)] * 3,
        scratch_shapes=[
            pltpu.VMEM((length, 2 * head), F32),
            pltpu.VMEM((length, PROMPT_ROWS), F32),
            pltpu.VMEM((length, PROMPT_ROWS), BF16),
        ],
        compiler_params=pltpu.CompilerParams(vmem_limit_bytes=28 * 1024 * 1024),
        cost_estimate=pl.CostEstimate(flops=24 * rows * length * head, bytes_accessed=8 * length * head, transcendentals=0),
        name="prompt_pass",
    )(place, q, do, *caches, carried)


def reply_kernel(
    scaling, inner, other_count, other_order, scalars_ref, lengths_ref, owners_ref, q_ref, do_ref, own_ref, *refs
):
    caches, refs = refs[: -13 - inner], refs[-13 - inner :]
    out_ref, dq_ref, other_sum_ref, mine_sum_ref = refs[:4]
    own_pieces = refs[4 : 4 + inner]
    picks_ref, q_t_ref, do_t_ref, results, grad, own_grad, score_ref, weight_ref, slope_ref = refs[4 + inner :]
    others, mines = caches[:other_count], caches[other_count:]
    capacity, head = q_ref.shape
    length = grad.shape[0]
    slots = lengths_ref.shape[0]
    window = capacity // 2

    starts, ranks, counts = [], [], []
    total = jnp.int32(0)
    edges = [total]
    for of_mine in (False, True):
        place_now = jnp.int32(0)
        for s in range(slots):
            taken = (owners_ref[s] == scalars_ref[1]) == of_mine
            count = jnp.where(taken, lengths_ref[s], 0)
            starts.append(place_now)
            ranks.append(total)
            counts.append(count)
            place_now = place_now + lengths_ref[s]
            total = total + count
        total = (total + ROWS - 1) // ROWS * ROWS
        edges.append(total)

    def located(rank_of):
        place = jnp.full(rank_of.shape, -1, jnp.int32)
        start = jnp.zeros(rank_of.shape, jnp.int32)
        for s in range(2 * slots):
            inside = (rank_of >= ranks[s]) & (rank_of < ranks[s] + counts[s])
            place = jnp.where(inside, rank_of + (starts[s] - ranks[s]), place)
            start = jnp.where(inside, starts[s], start)
        return place, start

    spread = q_t_ref.shape[1]
    place_all, _ = located(lax.broadcasted_iota(jnp.int32, (1, spread), 1))
    picks_ref[...] = jnp.where(
        lax.broadcasted_iota(jnp.int32, (capacity, spread), 0) == place_all, 1.0, 0.0
    ).astype(BF16)
    q_t_ref[...] = dot(turned(q_ref[...]), picks_ref[...], 1, 0).astype(BF16)
    do_t_ref[...] = dot(turned(do_ref[...]), picks_ref[...], 1, 0).astype(BF16)
    results[...] = jnp.zeros_like(results)
    own_grad[...] = jnp.zeros_like(own_grad)

    for parts, sum_ref, edge in ((others, other_sum_ref, 0), (mines, mine_sum_ref, 1)):
        grad[...] = jnp.zeros_like(grad)

        def block(b, unused):
            first_rank = pl.multiple_of(b * ROWS, ROWS)
            here = pl.ds(first_rank, ROWS)
            low, high = jnp.int32(capacity), jnp.int32(0)
            for s in range(2 * slots):
                begin = jnp.maximum(ranks[s], first_rank)
                end = jnp.minimum(ranks[s] + counts[s], first_rank + ROWS)
                some = begin < end
                low = jnp.where(some, jnp.minimum(low, starts[s]), low)
                high = jnp.where(some, jnp.maximum(high, end + (starts[s] - ranks[s])), high)
            low = (low // 32) * 32
            place, start = located(first_rank + lax.broadcasted_iota(jnp.int32, (1, ROWS), 1))

            def own_piece(w):
                begin = low + w * window
                at = pl.multiple_of(jnp.minimum(begin, capacity - window), 32)

                def packed(scores):
                    keys = at + lax.broadcasted_iota(jnp.int32, scores.shape, 0)
                    return jnp.where((keys >= jnp.maximum(start, begin)) & (keys <= place), scores, MASKED)

                return own_ref, at, own_grad, at, length + w * window, window, packed

            pieces, at = [], 0
            for cache_ref in parts:
                for begin in range(0, cache_ref.shape[0], CHUNK):
                    size = min(CHUNK, cache_ref.shape[0] - begin)
                    pieces.append((cache_ref, begin, grad, at, at, size, None))
                    at += size
            pieces.append(own_piece(0))
            extra = ((high - low + window - 1) // window, own_piece)
            out, query_grad = run_block(
                q_t_ref[:, here], do_t_ref[:, here], scaling, pieces, extra, score_ref, weight_ref, slope_ref
            )
            results[here, :head] = turned(out)
            results[here, head:] = turned(query_grad)
            return unused

        lax.fori_loop(edges[edge] // ROWS, edges[edge + 1] // ROWS, block, 0)
        if edge == 0:
            leave_in_order(scalars_ref[0], inner, length // (2 * inner), other_order, grad, sum_ref)
        else:
            sum_ref[...] = grad[...].astype(BF16)

    placed = dot(picks_ref[...], results[...], 1, 0).astype(BF16)
    out_ref[...] = placed[:, :head]
    dq_ref[...] = placed[:, head:]
    share = capacity // (2 * inner)
    for k, ref in enumerate(own_pieces):
        there = lax.rem(lax.rem(scalars_ref[0], inner) + k, inner)
        for outer in range(2):
            at = pl.multiple_of((outer * inner + there) * share, share)
            ref[outer * share : (outer + 1) * share, :] = own_grad[pl.ds(at, share), :].astype(BF16)


def reply_pass(scalars, inner, lengths, owners, q, do, own, others, other_order, mines, scaling):
    capacity, head = q.shape
    length = sum(part.shape[0] for part in mines)
    spread = capacity + ROWS
    return pl.pallas_call(
        functools.partial(reply_kernel, scaling, inner, len(others), other_order),
        out_shape=[
            jax.ShapeDtypeStruct((capacity, head), BF16),
            jax.ShapeDtypeStruct((capacity, head), BF16),
            jax.ShapeDtypeStruct((length, 2 * head), BF16),
            jax.ShapeDtypeStruct((length, 2 * head), BF16),
        ]
        + [jax.ShapeDtypeStruct((capacity // inner, 2 * head), BF16)] * inner,
        in_specs=[pl.BlockSpec(memory_space=pltpu.SMEM)] * 3 + [pl.BlockSpec(memory_space=pltpu.VMEM)] * (3 + len(others) + len(mines)),
        out_specs=[pl.BlockSpec(memory_space=pltpu.VMEM)] * (4 + inner),
        scratch_shapes=[
            pltpu.VMEM((capacity, spread), BF16),
            pltpu.VMEM((head, spread), BF16),
            pltpu.VMEM((head, spread), BF16),
            pltpu.VMEM((spread, 2 * head), BF16),
            pltpu.VMEM((length, 2 * head), F32),
            pltpu.VMEM((capacity, 2 * head), F32),
            pltpu.VMEM((length + capacity, ROWS), F32),
            pltpu.VMEM((length + capacity, ROWS), BF16),
            pltpu.VMEM((length + capacity, ROWS), F32),
        ],
        compiler_params=pltpu.CompilerParams(vmem_limit_bytes=36 * 1024 * 1024),
        cost_estimate=pl.CostEstimate(flops=24 * capacity * length * head, bytes_accessed=16 * length * head, transcendentals=0),
        name="reply_pass",
    )(scalars, lengths, owners, q, do, own, *others, *mines)


def place_kernel(inner, place_ref, *refs):
    out_ref = refs[-1]
    share = out_ref.shape[0] // (2 * inner)
    for k, ref in enumerate(refs[:-1]):
        there = lax.rem(lax.rem(place_ref[0], inner) + (inner - k), inner)
        for outer in range(2):
            at = pl.multiple_of((outer * inner + there) * share, share)
            out_ref[pl.ds(at, share), :] = ref[outer * share : (outer + 1) * share, :]


def placed_in_order(place, pieces):
    rows, width = pieces[0].shape
    return pl.pallas_call(
        functools.partial(place_kernel, len(pieces)),
        out_shape=jax.ShapeDtypeStruct((len(pieces) * rows, width), BF16),
        in_specs=[pl.BlockSpec(memory_space=pltpu.SMEM)] + [pl.BlockSpec(memory_space=pltpu.VMEM)] * len(pieces),
        out_specs=pl.BlockSpec(memory_space=pltpu.VMEM),
        compiler_params=pltpu.CompilerParams(vmem_limit_bytes=8 * 1024 * 1024),
        name="placed_in_order",
    )(place, *pieces)


def join_kernel(total_ref, arrived_ref, *refs):
    *pieces, shares_ref, part_ref = refs
    shares_ref[...] = (total_ref[...].astype(F32) + arrived_ref[...].astype(F32)).astype(BF16)
    part = pieces[0][...].astype(F32)
    for ref in pieces[1:]:
        part = part + ref[...].astype(F32)
    part_ref[...] = part.astype(BF16)


def join(total, arrived, pieces):
    return pl.pallas_call(
        join_kernel,
        out_shape=[jax.ShapeDtypeStruct(total.shape, BF16), jax.ShapeDtypeStruct(pieces[0].shape, BF16)],
        in_specs=[pl.BlockSpec(memory_space=pltpu.VMEM)] * (2 + len(pieces)),
        out_specs=[pl.BlockSpec(memory_space=pltpu.VMEM)] * 2,
        compiler_params=pltpu.CompilerParams(vmem_limit_bytes=16 * 1024 * 1024),
        name="join_sums",
    )(total, arrived, *pieces)


def per_device(
    prompt_query,
    prompt_cache,
    prompt_cotangent,
    reply_query,
    reply_cache,
    reply_cotangent,
    reply_lengths,
    reply_owner,
):
    width = prompt_cache.shape[2]
    scaling = (width // 2) ** (-0.5)
    capacity = reply_query.shape[0]
    ctx_count, comp_count, group_count = (lax.axis_size(name) for name in ("ctx", "comp", "grp"))
    inner, comp_inner = ctx_count // 2, comp_count // 2
    place = lax.axis_index("ctx").astype(jnp.int32).reshape(1)
    group = lax.axis_index("grp").astype(jnp.int32).reshape(1)

    def swap(x):
        return lax.ppermute(x, "grp", [(0, 1), (1, 0)])

    def along_z(x, k):
        pairs = [(i, i // inner * inner + (i + k) % inner) for i in range(ctx_count)]
        return lax.ppermute(x, "ctx", pairs)

    def outer_swap(x):
        return lax.ppermute(x, "ctx", [(i, (i + inner) % ctx_count) for i in range(ctx_count)])

    def along_y(x, k):
        pairs = []
        for ctx in range(ctx_count):
            for comp in range(comp_count):
                y = (2 * (comp // comp_inner) + ctx // inner + k) % 4
                to_ctx = y % 2 * inner + ctx % inner
                to_comp = y // 2 * comp_inner + comp % comp_inner
                pairs.append((ctx * comp_count + comp, to_ctx * comp_count + to_comp))
        return lax.ppermute(x, ("ctx", "comp"), pairs)

    with jax.named_scope("gather_keys"):
        own = prompt_cache[0]
        next_1, next_3, next_2 = along_z(own, 1), along_z(own, inner - 1), along_z(own, 2)
        y_0 = along_y(own, 1)
        y_1, y_3 = along_y(next_1, 1), along_y(next_3, -1)
        half = own.shape[0] // 2
        y_2a, y_2b = along_y(next_2[:half], 1), along_y(next_2[half:], -1)
        mines = [own, next_1, next_2, next_3, y_0, y_1, y_2a, y_2b, y_3]
        early, late = [own, next_1, next_3], [next_2, y_0, y_1, y_2a, y_2b, y_3]
        others = [swap(jnp.concatenate(part, axis=0)) for part in (early, late)]
        other_order = (0, 1, 3, 2, 4, 5, 6, 7)

    with jax.named_scope("reply_rows"):
        reply_out, reply_dq, other_sum, mine_sum, *own_pieces = reply_pass(
            jnp.concatenate([place, group]), inner, reply_lengths[0], reply_owner[0], reply_query, reply_cotangent, reply_cache,
            others, other_order, mines, scaling,
        )
    arrived = swap(other_sum)
    with jax.named_scope("prompt_rows"):
        prompt_out, prompt_dq, total = prompt_pass(
            place, inner, prompt_query[0], prompt_cotangent[0], mines, mine_sum, scaling
        )

    with jax.named_scope("prompt_cache_sum"):
        count = ctx_count * comp_count
        came = [along_z(own_pieces[k], k) for k in range(1, inner)]
        shares, part = join(total, arrived, [own_pieces[0], *came])
        terms = lax.all_to_all(shares.reshape(count, -1, width), ("ctx", "comp"), 0, 0, tiled=True)
    with jax.named_scope("reply_cache_sum"):
        part = (part.astype(F32) + outer_swap(part).astype(F32)).astype(BF16)
        reply_grad = placed_in_order(place, [part] + [along_z(part, k) for k in range(1, inner)])
    with jax.named_scope("prompt_cache_halves"):
        summed = jnp.sum(terms.astype(F32), axis=0).astype(BF16)
        rows = summed.shape[0] // group_count
        first, second = summed[:rows], summed[rows:]
        is_first = group[0] == 0
        kept = jnp.where(is_first, first, second)
        came = swap(jnp.where(is_first, second, first))
        prompt_grad = jnp.where(is_first, jnp.stack([kept, came]), jnp.stack([came, kept]))
    return (
        prompt_out[None],
        prompt_dq[None],
        prompt_grad,
        reply_out,
        reply_dq,
        reply_grad,
    )


def solution(mesh):
    return jax.shard_map(
        per_device,
        mesh=mesh,
        in_specs=(
            P("grp", "ctx", "comp"),
            P("grp", "ctx", None),
            P("grp", "ctx", "comp"),
            P(("comp", "grp"), "ctx"),
            P(("comp", "grp"), None),
            P(("comp", "grp"), "ctx"),
            P(("comp", "grp"), None),
            P(("comp", "grp"), None),
        ),
        out_specs=(
            P("grp", "ctx", "comp"),
            P("grp", "ctx", "comp"),
            P(None, ("ctx", "comp", "grp"), None),
            P(("comp", "grp"), "ctx"),
            P(("comp", "grp"), "ctx"),
            P(("comp", "grp"), None),
        ),
        check_vma=False,
    )
```

```python
import functools
import jax
import jax.numpy as jnp
from jax import lax
from jax.experimental import pallas as pl
from jax.experimental.pallas import tpu as pltpu
from jax.sharding import PartitionSpec as P

ROWS = 256
PROMPT_ROWS = 512
CHUNK = 512
LOG2E = 1.4426950408889634
MASKED = -1e30
F32 = jnp.float32
BF16 = jnp.bfloat16


def dot(a, b, ca, cb):
    return lax.dot_general(a, b, (((ca,), (cb,)), ((), ())), preferred_element_type=F32)


def turned(x):
    return x.astype(F32).T.astype(BF16)


def run_block(q_t, do_t, scaling, pieces, extra, score_ref, weight_ref, slope_ref=None):
    head, rows = q_t.shape
    steep = scaling * LOG2E

    def each(step, carry):
        for piece in pieces:
            carry = step(piece, carry)
        if extra is not None:
            carry = lax.fori_loop(1, extra[0], lambda w, c: step(extra[1](w), c), carry)
        return carry

    def scores_of(piece, highest):
        cache, at, _, _, row, size, mask = piece
        scores = dot(cache[pl.ds(at, size), :head], q_t, 1, 0)
        if mask is not None:
            scores = mask(scores)
        score_ref[pl.ds(row, size), :] = scores
        return jnp.maximum(highest, jnp.max(scores.reshape(size // 8, 8, rows), axis=0))

    highest = each(scores_of, jnp.full((8, rows), MASKED, F32))
    highest = jnp.max(highest, axis=0, keepdims=True) * steep

    def weights_of(piece, carry):
        cache, at, _, _, row, size, _ = piece
        total, out = carry
        weights = jnp.exp2(score_ref[pl.ds(row, size), :] * steep - highest)
        total = total + jnp.sum(weights.reshape(size // 8, 8, rows), axis=0)
        rounded = weights.astype(BF16)
        weight_ref[pl.ds(row, size), :] = rounded
        if slope_ref is not None:
            slope_ref[pl.ds(row, size), :] = dot(cache[pl.ds(at, size), head:], do_t, 1, 0)
        return total, out + dot(cache[pl.ds(at, size), head:], rounded, 0, 0)

    total, out = each(weights_of, (jnp.zeros((8, rows), F32), jnp.zeros((head, rows), F32)))
    inverse = 1.0 / jnp.sum(total, axis=0, keepdims=True)
    out = (out * inverse).astype(BF16)
    row_dot = jnp.sum(out.astype(F32) * do_t.astype(F32), axis=0, keepdims=True)
    q_scaled = turned(q_t.astype(F32) * (inverse * scaling))
    do_scaled = turned(do_t.astype(F32) * inverse)

    def grads_of(piece, query_grad):
        cache, at, grad, to, row, size, _ = piece
        rounded = weight_ref[pl.ds(row, size), :]
        if slope_ref is not None:
            weight_grad = slope_ref[pl.ds(row, size), :]
        else:
            weight_grad = dot(cache[pl.ds(at, size), head:], do_t, 1, 0)
        score_grad = (rounded.astype(F32) * (weight_grad - row_dot)).astype(BF16)
        grad[pl.ds(to, size), :head] += dot(score_grad, q_scaled, 1, 0)
        grad[pl.ds(to, size), head:] += dot(rounded, do_scaled, 1, 0)
        return query_grad + dot(cache[pl.ds(at, size), :head], score_grad, 0, 0)

    query_grad = each(grads_of, jnp.zeros((head, rows), F32))
    return out, (query_grad * (inverse * scaling)).astype(BF16)


def leave_in_order(me, inner, rows_here, order, grad, sum_ref):
    for i, k in enumerate(order):
        outer = lax.div(me, inner) if k < inner else 1 - lax.div(me, inner)
        place = outer * inner + lax.rem(lax.rem(me, inner) + (2 * inner - k), inner)
        at = pl.multiple_of(place * rows_here, rows_here)
        sum_ref[pl.ds(at, rows_here), :] = grad[i * rows_here : (i + 1) * rows_here, :].astype(BF16)


def prompt_kernel(scaling, inner, place_ref, q_ref, do_ref, *refs):
    caches, (carried_ref, out_ref, dq_ref, sum_ref, grad, score_ref, weight_ref) = refs[:-7], refs[-7:]
    length, rows_here = grad.shape[0], q_ref.shape[0]
    half = length // 2
    me_outer, me_inner = lax.div(place_ref[0], inner), lax.rem(place_ref[0], inner)
    grad[...] = carried_ref[...].astype(F32)

    def block(b, unused):
        here = pl.multiple_of(b * PROMPT_ROWS, PROMPT_ROWS)

        def causal(scores):
            keys = lax.broadcasted_iota(jnp.int32, scores.shape, 0)
            rows = here + lax.broadcasted_iota(jnp.int32, scores.shape, 1)
            return jnp.where(keys <= rows, scores, MASKED)

        def earlier(at, scores):
            keys = at + lax.broadcasted_iota(jnp.int32, scores.shape, 0)
            limit = rows_here * (me_inner + 1) if at < half else length * me_outer
            return jnp.where(keys < limit, scores, MASKED)

        pieces, at = [], 0
        for cache_ref in caches:
            begin = 0
            while begin < cache_ref.shape[0]:
                size = rows_here if at == 0 else min(CHUNK, cache_ref.shape[0] - begin)
                mask = causal if at == 0 else functools.partial(earlier, at)
                pieces.append((cache_ref, begin, grad, at, at, size, mask))
                at, begin = at + size, begin + size
        out, query_grad = run_block(
            turned(q_ref[pl.ds(here, PROMPT_ROWS), :]), turned(do_ref[pl.ds(here, PROMPT_ROWS), :]), scaling, pieces, None, score_ref, weight_ref
        )
        out_ref[pl.ds(here, PROMPT_ROWS), :] = turned(out)
        dq_ref[pl.ds(here, PROMPT_ROWS), :] = turned(query_grad)
        return unused

    lax.fori_loop(0, rows_here // PROMPT_ROWS, block, 0)
    leave_in_order(place_ref[0], inner, rows_here, range(2 * inner), grad, sum_ref)


def prompt_pass(place, inner, q, do, caches, carried, scaling):
    rows, head = q.shape
    length = carried.shape[0]
    return pl.pallas_call(
        functools.partial(prompt_kernel, scaling, inner),
        out_shape=[
            jax.ShapeDtypeStruct((rows, head), BF16),
            jax.ShapeDtypeStruct((rows, head), BF16),
            jax.ShapeDtypeStruct((length, 2 * head), BF16),
        ],
        in_specs=[pl.BlockSpec(memory_space=pltpu.SMEM)] + [pl.BlockSpec(memory_space=pltpu.VMEM)] * (3 + len(caches)),
        out_specs=[pl.BlockSpec(memory_space=pltpu.VMEM)] * 3,
        scratch_shapes=[
            pltpu.VMEM((length, 2 * head), F32),
            pltpu.VMEM((length, PROMPT_ROWS), F32),
            pltpu.VMEM((length, PROMPT_ROWS), BF16),
        ],
        compiler_params=pltpu.CompilerParams(vmem_limit_bytes=28 * 1024 * 1024),
        cost_estimate=pl.CostEstimate(flops=24 * rows * length * head, bytes_accessed=8 * length * head, transcendentals=0),
        name="prompt_pass",
    )(place, q, do, *caches, carried)


def ranking(scalars_ref, lengths_ref, owners_ref):
    slots = lengths_ref.shape[0]
    starts, ranks, counts = [], [], []
    total = jnp.int32(0)
    edges = [total]
    for of_mine in (False, True):
        place_now = jnp.int32(0)
        for s in range(slots):
            taken = (owners_ref[s] == scalars_ref[1]) == of_mine
            count = jnp.where(taken, lengths_ref[s], 0)
            starts.append(place_now)
            ranks.append(total)
            counts.append(count)
            place_now = place_now + lengths_ref[s]
            total = total + count
        total = (total + ROWS - 1) // ROWS * ROWS
        edges.append(total)

    def located(rank_of):
        place = jnp.full(rank_of.shape, -1, jnp.int32)
        start = jnp.zeros(rank_of.shape, jnp.int32)
        for s in range(2 * slots):
            inside = (rank_of >= ranks[s]) & (rank_of < ranks[s] + counts[s])
            place = jnp.where(inside, rank_of + (starts[s] - ranks[s]), place)
            start = jnp.where(inside, starts[s], start)
        return place, start

    return starts, ranks, counts, edges, located


def order_kernel(scalars_ref, lengths_ref, owners_ref, q_ref, do_ref, own_ref, picks_ref, q_t_ref, do_t_ref, staged_ref):
    _, _, _, _, located = ranking(scalars_ref, lengths_ref, owners_ref)
    place, _ = located(lax.broadcasted_iota(jnp.int32, (1, picks_ref.shape[1]), 1))
    picks_ref[...] = jnp.where(
        lax.broadcasted_iota(jnp.int32, picks_ref.shape, 0) == place, 1.0, 0.0
    ).astype(BF16)
    q_t_ref[...] = dot(turned(q_ref[...]), picks_ref[...], 1, 0).astype(BF16)
    do_t_ref[...] = dot(turned(do_ref[...]), picks_ref[...], 1, 0).astype(BF16)
    staged_ref[...] = own_ref[...]


def order_rows(scalars, lengths, owners, q, do, own):
    capacity, head = q.shape
    spread = capacity + ROWS
    return pl.pallas_call(
        order_kernel,
        out_shape=[
            jax.ShapeDtypeStruct((capacity, spread), BF16),
            jax.ShapeDtypeStruct((head, spread), BF16),
            jax.ShapeDtypeStruct((head, spread), BF16),
            jax.ShapeDtypeStruct(own.shape, BF16),
        ],
        in_specs=[pl.BlockSpec(memory_space=pltpu.SMEM)] * 3 + [pl.BlockSpec(memory_space=pltpu.VMEM)] * 3,
        out_specs=[pl.BlockSpec(memory_space=pltpu.VMEM)] * 4,
        compiler_params=pltpu.CompilerParams(vmem_limit_bytes=16 * 1024 * 1024),
        cost_estimate=pl.CostEstimate(flops=4 * capacity * spread * head, bytes_accessed=8 * capacity * spread, transcendentals=0),
        name="order_rows",
    )(scalars, lengths, owners, q, do, own)


def stack_kernel(after_ref, *refs):
    *pieces, out_ref = refs
    at = 0
    for ref in pieces:
        out_ref[at : at + ref.shape[0], :] = ref[...]
        at += ref.shape[0]


def stack_after(after, pieces):
    rows = sum(x.shape[0] for x in pieces)
    return pl.pallas_call(
        stack_kernel,
        out_shape=jax.ShapeDtypeStruct((rows, pieces[0].shape[1]), BF16),
        in_specs=[pl.BlockSpec(memory_space=pl.ANY)] + [pl.BlockSpec(memory_space=pltpu.VMEM)] * len(pieces),
        out_specs=pl.BlockSpec(memory_space=pltpu.VMEM),
        compiler_params=pltpu.CompilerParams(vmem_limit_bytes=8 * 1024 * 1024),
        name="stack_after",
    )(after, *pieces)


def reply_kernel(
    scaling, inner, other_count, other_order, scalars_ref, lengths_ref, owners_ref, picks_ref, q_t_ref, do_t_ref, own_ref, *refs
):
    caches, refs = refs[: -10 - inner], refs[-10 - inner :]
    out_ref, dq_ref, other_sum_ref, mine_sum_ref = refs[:4]
    own_pieces = refs[4 : 4 + inner]
    results, grad, own_grad, score_ref, weight_ref, slope_ref = refs[4 + inner :]
    others, mines = caches[:other_count], caches[other_count:]
    capacity, head = own_ref.shape[0], own_ref.shape[1] // 2
    length = grad.shape[0]
    slots = lengths_ref.shape[0]
    window = capacity // 2

    starts, ranks, counts, edges, located = ranking(scalars_ref, lengths_ref, owners_ref)
    results[...] = jnp.zeros_like(results)
    own_grad[...] = jnp.zeros_like(own_grad)

    for parts, sum_ref, edge in ((others, other_sum_ref, 0), (mines, mine_sum_ref, 1)):
        grad[...] = jnp.zeros_like(grad)

        def block(b, unused):
            first_rank = pl.multiple_of(b * ROWS, ROWS)
            here = pl.ds(first_rank, ROWS)
            low, high = jnp.int32(capacity), jnp.int32(0)
            for s in range(2 * slots):
                begin = jnp.maximum(ranks[s], first_rank)
                end = jnp.minimum(ranks[s] + counts[s], first_rank + ROWS)
                some = begin < end
                low = jnp.where(some, jnp.minimum(low, starts[s]), low)
                high = jnp.where(some, jnp.maximum(high, end + (starts[s] - ranks[s])), high)
            low = (low // 32) * 32
            place, start = located(first_rank + lax.broadcasted_iota(jnp.int32, (1, ROWS), 1))

            def own_piece(w):
                begin = low + w * window
                at = pl.multiple_of(jnp.minimum(begin, capacity - window), 32)

                def packed(scores):
                    keys = at + lax.broadcasted_iota(jnp.int32, scores.shape, 0)
                    return jnp.where((keys >= jnp.maximum(start, begin)) & (keys <= place), scores, MASKED)

                return own_ref, at, own_grad, at, length + w * window, window, packed

            pieces, at = [], 0
            for cache_ref in parts:
                for begin in range(0, cache_ref.shape[0], CHUNK):
                    size = min(CHUNK, cache_ref.shape[0] - begin)
                    pieces.append((cache_ref, begin, grad, at, at, size, None))
                    at += size
            pieces.append(own_piece(0))
            extra = ((high - low + window - 1) // window, own_piece)
            out, query_grad = run_block(
                q_t_ref[:, here], do_t_ref[:, here], scaling, pieces, extra, score_ref, weight_ref, slope_ref
            )
            results[here, :head] = turned(out)
            results[here, head:] = turned(query_grad)
            return unused

        lax.fori_loop(edges[edge] // ROWS, edges[edge + 1] // ROWS, block, 0)
        if edge == 0:
            leave_in_order(scalars_ref[0], inner, length // (2 * inner), other_order, grad, sum_ref)
        else:
            sum_ref[...] = grad[...].astype(BF16)

    placed = dot(picks_ref[...], results[...], 1, 0).astype(BF16)
    out_ref[...] = placed[:, :head]
    dq_ref[...] = placed[:, head:]
    share = capacity // (2 * inner)
    for k, ref in enumerate(own_pieces):
        there = lax.rem(lax.rem(scalars_ref[0], inner) + k, inner)
        for outer in range(2):
            at = pl.multiple_of((outer * inner + there) * share, share)
            ref[outer * share : (outer + 1) * share, :] = own_grad[pl.ds(at, share), :].astype(BF16)


def reply_pass(scalars, inner, lengths, owners, ordered, others, other_order, mines, scaling):
    capacity, head = ordered[3].shape[0], ordered[3].shape[1] // 2
    length = sum(part.shape[0] for part in mines)
    spread = capacity + ROWS
    return pl.pallas_call(
        functools.partial(reply_kernel, scaling, inner, len(others), other_order),
        out_shape=[
            jax.ShapeDtypeStruct((capacity, head), BF16),
            jax.ShapeDtypeStruct((capacity, head), BF16),
            jax.ShapeDtypeStruct((length, 2 * head), BF16),
            jax.ShapeDtypeStruct((length, 2 * head), BF16),
        ]
        + [jax.ShapeDtypeStruct((capacity // inner, 2 * head), BF16)] * inner,
        in_specs=[pl.BlockSpec(memory_space=pltpu.SMEM)] * 3 + [pl.BlockSpec(memory_space=pltpu.VMEM)] * (len(ordered) + len(others) + len(mines)),
        out_specs=[pl.BlockSpec(memory_space=pltpu.VMEM)] * (4 + inner),
        scratch_shapes=[
            pltpu.VMEM((spread, 2 * head), BF16),
            pltpu.VMEM((length, 2 * head), F32),
            pltpu.VMEM((capacity, 2 * head), F32),
            pltpu.VMEM((length + capacity, ROWS), F32),
            pltpu.VMEM((length + capacity, ROWS), BF16),
            pltpu.VMEM((length + capacity, ROWS), F32),
        ],
        compiler_params=pltpu.CompilerParams(vmem_limit_bytes=36 * 1024 * 1024),
        cost_estimate=pl.CostEstimate(flops=24 * capacity * length * head, bytes_accessed=16 * length * head, transcendentals=0),
        name="reply_pass",
    )(scalars, lengths, owners, *ordered, *others, *mines)


def place_kernel(inner, place_ref, *refs):
    out_ref = refs[-1]
    share = out_ref.shape[0] // (2 * inner)
    for k, ref in enumerate(refs[:-1]):
        there = lax.rem(lax.rem(place_ref[0], inner) + (inner - k), inner)
        for outer in range(2):
            at = pl.multiple_of((outer * inner + there) * share, share)
            out_ref[pl.ds(at, share), :] = ref[outer * share : (outer + 1) * share, :]


def placed_in_order(place, pieces):
    rows, width = pieces[0].shape
    return pl.pallas_call(
        functools.partial(place_kernel, len(pieces)),
        out_shape=jax.ShapeDtypeStruct((len(pieces) * rows, width), BF16),
        in_specs=[pl.BlockSpec(memory_space=pltpu.SMEM)] + [pl.BlockSpec(memory_space=pltpu.VMEM)] * len(pieces),
        out_specs=pl.BlockSpec(memory_space=pltpu.VMEM),
        compiler_params=pltpu.CompilerParams(vmem_limit_bytes=8 * 1024 * 1024),
        name="placed_in_order",
    )(place, *pieces)


def join_kernel(total_ref, arrived_ref, *refs):
    *pieces, shares_ref, part_ref = refs
    shares_ref[...] = (total_ref[...].astype(F32) + arrived_ref[...].astype(F32)).astype(BF16)
    part = pieces[0][...].astype(F32)
    for ref in pieces[1:]:
        part = part + ref[...].astype(F32)
    part_ref[...] = part.astype(BF16)


def join(total, arrived, pieces):
    return pl.pallas_call(
        join_kernel,
        out_shape=[jax.ShapeDtypeStruct(total.shape, BF16), jax.ShapeDtypeStruct(pieces[0].shape, BF16)],
        in_specs=[pl.BlockSpec(memory_space=pltpu.VMEM)] * (2 + len(pieces)),
        out_specs=[pl.BlockSpec(memory_space=pltpu.VMEM)] * 2,
        compiler_params=pltpu.CompilerParams(vmem_limit_bytes=16 * 1024 * 1024),
        name="join_sums",
    )(total, arrived, *pieces)


def per_device(
    prompt_query,
    prompt_cache,
    prompt_cotangent,
    reply_query,
    reply_cache,
    reply_cotangent,
    reply_lengths,
    reply_owner,
):
    width = prompt_cache.shape[2]
    scaling = (width // 2) ** (-0.5)
    capacity = reply_query.shape[0]
    ctx_count, comp_count, group_count = (lax.axis_size(name) for name in ("ctx", "comp", "grp"))
    inner, comp_inner = ctx_count // 2, comp_count // 2
    place = lax.axis_index("ctx").astype(jnp.int32).reshape(1)
    group = lax.axis_index("grp").astype(jnp.int32).reshape(1)

    def swap(x):
        return lax.ppermute(x, "grp", [(0, 1), (1, 0)])

    def along_z(x, k):
        pairs = [(i, i // inner * inner + (i + k) % inner) for i in range(ctx_count)]
        return lax.ppermute(x, "ctx", pairs)

    def outer_swap(x):
        return lax.ppermute(x, "ctx", [(i, (i + inner) % ctx_count) for i in range(ctx_count)])

    def along_y(x, k):
        pairs = []
        for ctx in range(ctx_count):
            for comp in range(comp_count):
                y = (2 * (comp // comp_inner) + ctx // inner + k) % 4
                to_ctx = y % 2 * inner + ctx % inner
                to_comp = y // 2 * comp_inner + comp % comp_inner
                pairs.append((ctx * comp_count + comp, to_ctx * comp_count + to_comp))
        return lax.ppermute(x, ("ctx", "comp"), pairs)

    reply_scalars = (jnp.concatenate([place, group]), reply_lengths[0], reply_owner[0])
    with jax.named_scope("order_rows"):
        ordered = order_rows(*reply_scalars, reply_query, reply_cotangent, reply_cache)
    with jax.named_scope("gather_keys"):
        own = prompt_cache[0]
        next_1, next_3 = along_z(own, 1), along_z(own, inner - 1)
        y_0 = along_y(own, 1)
        half = own.shape[0] // 2
        next_2a, next_2b = along_z(next_1[:half], 1), along_z(next_3[half:], inner - 1)
        y_1, y_3 = along_y(next_1, 1), along_y(next_3, -1)
        y_2a, y_2b = along_y(next_2a, 1), along_y(next_2b, -1)
        mines = [own, next_1, next_2a, next_2b, next_3, y_0, y_1, y_2a, y_2b, y_3]
        early, late = [own, next_1, next_3], [next_2a, next_2b, y_0, y_1, y_2a, y_2b, y_3]
        others = [swap(jnp.concatenate(early, axis=0)), swap(stack_after(ordered[3], late))]
        other_order = (0, 1, 3, 2, 4, 5, 6, 7)

    with jax.named_scope("reply_rows"):
        scalars, lengths, owners = reply_scalars
        reply_out, reply_dq, other_sum, mine_sum, *own_pieces = reply_pass(
            scalars, inner, lengths, owners, ordered, others, other_order, mines, scaling
        )
    arrived = swap(other_sum)
    with jax.named_scope("prompt_rows"):
        prompt_out, prompt_dq, total = prompt_pass(
            place, inner, prompt_query[0], prompt_cotangent[0], mines, mine_sum, scaling
        )

    with jax.named_scope("prompt_cache_sum"):
        count = ctx_count * comp_count
        came = [along_z(own_pieces[k], k) for k in range(1, inner)]
        shares, part = join(total, arrived, [own_pieces[0], *came])
        terms = lax.all_to_all(shares.reshape(count, -1, width), ("ctx", "comp"), 0, 0, tiled=True)
    with jax.named_scope("reply_cache_sum"):
        part = (part.astype(F32) + outer_swap(part).astype(F32)).astype(BF16)
        reply_grad = placed_in_order(place, [part] + [along_z(part, k) for k in range(1, inner)])
    with jax.named_scope("prompt_cache_halves"):
        summed = jnp.sum(terms.astype(F32), axis=0).astype(BF16)
        rows = summed.shape[0] // group_count
        first, second = summed[:rows], summed[rows:]
        is_first = group[0] == 0
        kept = jnp.where(is_first, first, second)
        came = swap(jnp.where(is_first, second, first))
        prompt_grad = jnp.where(is_first, jnp.stack([kept, came]), jnp.stack([came, kept]))
    return (
        prompt_out[None],
        prompt_dq[None],
        prompt_grad,
        reply_out,
        reply_dq,
        reply_grad,
    )


def solution(mesh):
    return jax.shard_map(
        per_device,
        mesh=mesh,
        in_specs=(
            P("grp", "ctx", "comp"),
            P("grp", "ctx", None),
            P("grp", "ctx", "comp"),
            P(("comp", "grp"), "ctx"),
            P(("comp", "grp"), None),
            P(("comp", "grp"), "ctx"),
            P(("comp", "grp"), None),
            P(("comp", "grp"), None),
        ),
        out_specs=(
            P("grp", "ctx", "comp"),
            P("grp", "ctx", "comp"),
            P(None, ("ctx", "comp", "grp"), None),
            P(("comp", "grp"), "ctx"),
            P(("comp", "grp"), "ctx"),
            P(("comp", "grp"), None),
        ),
        check_vma=False,
    )
```

```python
import functools
import jax
import jax.numpy as jnp
from jax import lax
from jax.experimental import pallas as pl
from jax.experimental.pallas import tpu as pltpu
from jax.sharding import PartitionSpec as P

ROWS = 256
PROMPT_ROWS = 512
CHUNK = 512
LOG2E = 1.4426950408889634
MASKED = -1e30
F32 = jnp.float32
BF16 = jnp.bfloat16


def dot(a, b, ca, cb):
    return lax.dot_general(a, b, (((ca,), (cb,)), ((), ())), preferred_element_type=F32)


def turned(x):
    return x.astype(F32).T.astype(BF16)


def run_block(q_t, do_t, scaling, pieces, extra, score_ref, weight_ref, slope_ref=None):
    head, rows = q_t.shape
    steep = scaling * LOG2E

    def each(step, carry):
        for piece in pieces:
            carry = step(piece, carry)
        if extra is not None:
            carry = lax.fori_loop(1, extra[0], lambda w, c: step(extra[1](w), c), carry)
        return carry

    def scores_of(piece, highest):
        cache, at, _, _, row, size, mask = piece
        scores = dot(cache[pl.ds(at, size), :head], q_t, 1, 0)
        if mask is not None:
            scores = mask(scores)
        score_ref[pl.ds(row, size), :] = scores
        return jnp.maximum(highest, jnp.max(scores.reshape(size // 8, 8, rows), axis=0))

    highest = each(scores_of, jnp.full((8, rows), MASKED, F32))
    highest = jnp.max(highest, axis=0, keepdims=True) * steep

    def weights_of(piece, carry):
        cache, at, _, _, row, size, _ = piece
        total, out = carry
        weights = jnp.exp2(score_ref[pl.ds(row, size), :] * steep - highest)
        total = total + jnp.sum(weights.reshape(size // 8, 8, rows), axis=0)
        rounded = weights.astype(BF16)
        weight_ref[pl.ds(row, size), :] = rounded
        if slope_ref is not None:
            slope_ref[pl.ds(row, size), :] = dot(cache[pl.ds(at, size), head:], do_t, 1, 0)
        return total, out + dot(cache[pl.ds(at, size), head:], rounded, 0, 0)

    total, out = each(weights_of, (jnp.zeros((8, rows), F32), jnp.zeros((head, rows), F32)))
    inverse = 1.0 / jnp.sum(total, axis=0, keepdims=True)
    out = (out * inverse).astype(BF16)
    row_dot = jnp.sum(out.astype(F32) * do_t.astype(F32), axis=0, keepdims=True)
    q_scaled = turned(q_t.astype(F32) * (inverse * scaling))
    do_scaled = turned(do_t.astype(F32) * inverse)

    def grads_of(piece, query_grad):
        cache, at, grad, to, row, size, _ = piece
        rounded = weight_ref[pl.ds(row, size), :]
        if slope_ref is not None:
            weight_grad = slope_ref[pl.ds(row, size), :]
        else:
            weight_grad = dot(cache[pl.ds(at, size), head:], do_t, 1, 0)
        score_grad = (rounded.astype(F32) * (weight_grad - row_dot)).astype(BF16)
        grad[pl.ds(to, size), :head] += dot(score_grad, q_scaled, 1, 0)
        grad[pl.ds(to, size), head:] += dot(rounded, do_scaled, 1, 0)
        return query_grad + dot(cache[pl.ds(at, size), :head], score_grad, 0, 0)

    query_grad = each(grads_of, jnp.zeros((head, rows), F32))
    return out, (query_grad * (inverse * scaling)).astype(BF16)


def leave_in_order(me, inner, rows_here, order, grad, sum_ref):
    for i, k in enumerate(order):
        outer = lax.div(me, inner) if k < inner else 1 - lax.div(me, inner)
        place = outer * inner + lax.rem(lax.rem(me, inner) + (2 * inner - k), inner)
        at = pl.multiple_of(place * rows_here, rows_here)
        sum_ref[pl.ds(at, rows_here), :] = grad[i * rows_here : (i + 1) * rows_here, :].astype(BF16)


def prompt_kernel(scaling, inner, place_ref, q_ref, do_ref, *refs):
    caches, (carried_ref, out_ref, dq_ref, sum_ref, grad, score_ref, weight_ref) = refs[:-7], refs[-7:]
    length, rows_here = grad.shape[0], q_ref.shape[0]
    half = length // 2
    me_outer, me_inner = lax.div(place_ref[0], inner), lax.rem(place_ref[0], inner)
    grad[...] = carried_ref[...].astype(F32)

    def block(b, unused):
        here = pl.multiple_of(b * PROMPT_ROWS, PROMPT_ROWS)

        def causal(scores):
            keys = lax.broadcasted_iota(jnp.int32, scores.shape, 0)
            rows = here + lax.broadcasted_iota(jnp.int32, scores.shape, 1)
            return jnp.where(keys <= rows, scores, MASKED)

        def earlier(at, scores):
            keys = at + lax.broadcasted_iota(jnp.int32, scores.shape, 0)
            limit = rows_here * (me_inner + 1) if at < half else length * me_outer
            return jnp.where(keys < limit, scores, MASKED)

        pieces, at = [], 0
        for cache_ref in caches:
            begin = 0
            while begin < cache_ref.shape[0]:
                size = rows_here if at == 0 else min(CHUNK, cache_ref.shape[0] - begin)
                mask = causal if at == 0 else functools.partial(earlier, at)
                pieces.append((cache_ref, begin, grad, at, at, size, mask))
                at, begin = at + size, begin + size
        out, query_grad = run_block(
            turned(q_ref[pl.ds(here, PROMPT_ROWS), :]), turned(do_ref[pl.ds(here, PROMPT_ROWS), :]), scaling, pieces, None, score_ref, weight_ref
        )
        out_ref[pl.ds(here, PROMPT_ROWS), :] = turned(out)
        dq_ref[pl.ds(here, PROMPT_ROWS), :] = turned(query_grad)
        return unused

    lax.fori_loop(0, rows_here // PROMPT_ROWS, block, 0)
    leave_in_order(place_ref[0], inner, rows_here, range(2 * inner), grad, sum_ref)


def prompt_pass(place, inner, q, do, caches, carried, scaling):
    rows, head = q.shape
    length = carried.shape[0]
    return pl.pallas_call(
        functools.partial(prompt_kernel, scaling, inner),
        out_shape=[
            jax.ShapeDtypeStruct((rows, head), BF16),
            jax.ShapeDtypeStruct((rows, head), BF16),
            jax.ShapeDtypeStruct((length, 2 * head), BF16),
        ],
        in_specs=[pl.BlockSpec(memory_space=pltpu.SMEM)] + [pl.BlockSpec(memory_space=pltpu.VMEM)] * (3 + len(caches)),
        out_specs=[pl.BlockSpec(memory_space=pltpu.VMEM)] * 3,
        scratch_shapes=[
            pltpu.VMEM((length, 2 * head), F32),
            pltpu.VMEM((length, PROMPT_ROWS), F32),
            pltpu.VMEM((length, PROMPT_ROWS), BF16),
        ],
        compiler_params=pltpu.CompilerParams(vmem_limit_bytes=28 * 1024 * 1024),
        cost_estimate=pl.CostEstimate(flops=24 * rows * length * head, bytes_accessed=8 * length * head, transcendentals=0),
        name="prompt_pass",
    )(place, q, do, *caches, carried)


def ranking(scalars_ref, lengths_ref, owners_ref):
    slots = lengths_ref.shape[0]
    starts, ranks, counts = [], [], []
    total = jnp.int32(0)
    edges = [total]
    for of_mine in (False, True):
        place_now = jnp.int32(0)
        for s in range(slots):
            taken = (owners_ref[s] == scalars_ref[1]) == of_mine
            count = jnp.where(taken, lengths_ref[s], 0)
            starts.append(place_now)
            ranks.append(total)
            counts.append(count)
            place_now = place_now + lengths_ref[s]
            total = total + count
        total = (total + ROWS - 1) // ROWS * ROWS
        edges.append(total)

    def located(rank_of):
        place = jnp.full(rank_of.shape, -1, jnp.int32)
        start = jnp.zeros(rank_of.shape, jnp.int32)
        for s in range(2 * slots):
            inside = (rank_of >= ranks[s]) & (rank_of < ranks[s] + counts[s])
            place = jnp.where(inside, rank_of + (starts[s] - ranks[s]), place)
            start = jnp.where(inside, starts[s], start)
        return place, start

    return starts, ranks, counts, edges, located


def order_kernel(scalars_ref, lengths_ref, owners_ref, q_ref, do_ref, own_ref, picks_ref, q_t_ref, do_t_ref, staged_ref):
    _, _, _, _, located = ranking(scalars_ref, lengths_ref, owners_ref)
    place, _ = located(lax.broadcasted_iota(jnp.int32, (1, picks_ref.shape[1]), 1))
    picks_ref[...] = jnp.where(
        lax.broadcasted_iota(jnp.int32, picks_ref.shape, 0) == place, 1.0, 0.0
    ).astype(BF16)
    q_t_ref[...] = dot(turned(q_ref[...]), picks_ref[...], 1, 0).astype(BF16)
    do_t_ref[...] = dot(turned(do_ref[...]), picks_ref[...], 1, 0).astype(BF16)
    staged_ref[...] = own_ref[...]


def order_rows(scalars, lengths, owners, q, do, own):
    capacity, head = q.shape
    spread = capacity + ROWS
    return pl.pallas_call(
        order_kernel,
        out_shape=[
            jax.ShapeDtypeStruct((capacity, spread), BF16),
            jax.ShapeDtypeStruct((head, spread), BF16),
            jax.ShapeDtypeStruct((head, spread), BF16),
            jax.ShapeDtypeStruct(own.shape, BF16),
        ],
        in_specs=[pl.BlockSpec(memory_space=pltpu.SMEM)] * 3 + [pl.BlockSpec(memory_space=pltpu.VMEM)] * 3,
        out_specs=[pl.BlockSpec(memory_space=pltpu.VMEM)] * 4,
        compiler_params=pltpu.CompilerParams(vmem_limit_bytes=16 * 1024 * 1024),
        cost_estimate=pl.CostEstimate(flops=4 * capacity * spread * head, bytes_accessed=8 * capacity * spread, transcendentals=0),
        name="order_rows",
    )(scalars, lengths, owners, q, do, own)


def stack_kernel(after_ref, *refs):
    *pieces, out_ref = refs
    at = 0
    for ref in pieces:
        out_ref[at : at + ref.shape[0], :] = ref[...]
        at += ref.shape[0]


def stack_after(after, pieces):
    rows = sum(x.shape[0] for x in pieces)
    return pl.pallas_call(
        stack_kernel,
        out_shape=jax.ShapeDtypeStruct((rows, pieces[0].shape[1]), BF16),
        in_specs=[pl.BlockSpec(memory_space=pl.ANY)] + [pl.BlockSpec(memory_space=pltpu.VMEM)] * len(pieces),
        out_specs=pl.BlockSpec(memory_space=pltpu.VMEM),
        compiler_params=pltpu.CompilerParams(vmem_limit_bytes=8 * 1024 * 1024),
        name="stack_after",
    )(after, *pieces)


def reply_kernel(
    scaling, inner, other_count, other_order, scalars_ref, lengths_ref, owners_ref, picks_ref, q_t_ref, do_t_ref, own_ref, *refs
):
    caches, refs = refs[: -10 - inner], refs[-10 - inner :]
    out_ref, dq_ref, other_sum_ref, mine_sum_ref = refs[:4]
    own_pieces = refs[4 : 4 + inner]
    results, grad, own_grad, score_ref, weight_ref, slope_ref = refs[4 + inner :]
    others, mines = caches[:other_count], caches[other_count:]
    capacity, head = own_ref.shape[0], own_ref.shape[1] // 2
    length = grad.shape[0]
    slots = lengths_ref.shape[0]
    window = capacity // 2

    starts, ranks, counts, edges, located = ranking(scalars_ref, lengths_ref, owners_ref)
    results[...] = jnp.zeros_like(results)
    own_grad[...] = jnp.zeros_like(own_grad)

    for parts, sum_ref, edge in ((others, other_sum_ref, 0), (mines, mine_sum_ref, 1)):
        grad[...] = jnp.zeros_like(grad)

        def block(b, unused):
            first_rank = pl.multiple_of(b * ROWS, ROWS)
            here = pl.ds(first_rank, ROWS)
            low, high = jnp.int32(capacity), jnp.int32(0)
            for s in range(2 * slots):
                begin = jnp.maximum(ranks[s], first_rank)
                end = jnp.minimum(ranks[s] + counts[s], first_rank + ROWS)
                some = begin < end
                low = jnp.where(some, jnp.minimum(low, starts[s]), low)
                high = jnp.where(some, jnp.maximum(high, end + (starts[s] - ranks[s])), high)
            low = (low // 32) * 32
            place, start = located(first_rank + lax.broadcasted_iota(jnp.int32, (1, ROWS), 1))

            def own_piece(w):
                begin = low + w * window
                at = pl.multiple_of(jnp.minimum(begin, capacity - window), 32)

                def packed(scores):
                    keys = at + lax.broadcasted_iota(jnp.int32, scores.shape, 0)
                    return jnp.where((keys >= jnp.maximum(start, begin)) & (keys <= place), scores, MASKED)

                return own_ref, at, own_grad, at, length + w * window, window, packed

            pieces, at = [], 0
            for cache_ref in parts:
                for begin in range(0, cache_ref.shape[0], CHUNK):
                    size = min(CHUNK, cache_ref.shape[0] - begin)
                    pieces.append((cache_ref, begin, grad, at, at, size, None))
                    at += size
            pieces.append(own_piece(0))
            extra = ((high - low + window - 1) // window, own_piece)
            out, query_grad = run_block(
                q_t_ref[:, here], do_t_ref[:, here], scaling, pieces, extra, score_ref, weight_ref, slope_ref
            )
            results[here, :head] = turned(out)
            results[here, head:] = turned(query_grad)
            return unused

        lax.fori_loop(edges[edge] // ROWS, edges[edge + 1] // ROWS, block, 0)
        if edge == 0:
            leave_in_order(scalars_ref[0], inner, length // (2 * inner), other_order, grad, sum_ref)
        else:
            sum_ref[...] = grad[...].astype(BF16)

    placed = dot(picks_ref[...], results[...], 1, 0).astype(BF16)
    out_ref[...] = placed[:, :head]
    dq_ref[...] = placed[:, head:]
    share = capacity // (2 * inner)
    for k, ref in enumerate(own_pieces):
        there = lax.rem(lax.rem(scalars_ref[0], inner) + k, inner)
        for outer in range(2):
            at = pl.multiple_of((outer * inner + there) * share, share)
            ref[outer * share : (outer + 1) * share, :] = own_grad[pl.ds(at, share), :].astype(BF16)


def reply_pass(scalars, inner, lengths, owners, ordered, others, other_order, mines, scaling):
    capacity, head = ordered[3].shape[0], ordered[3].shape[1] // 2
    length = sum(part.shape[0] for part in mines)
    spread = capacity + ROWS
    return pl.pallas_call(
        functools.partial(reply_kernel, scaling, inner, len(others), other_order),
        out_shape=[
            jax.ShapeDtypeStruct((capacity, head), BF16),
            jax.ShapeDtypeStruct((capacity, head), BF16),
            jax.ShapeDtypeStruct((length, 2 * head), BF16),
            jax.ShapeDtypeStruct((length, 2 * head), BF16),
        ]
        + [jax.ShapeDtypeStruct((capacity // inner, 2 * head), BF16)] * inner,
        in_specs=[pl.BlockSpec(memory_space=pltpu.SMEM)] * 3 + [pl.BlockSpec(memory_space=pltpu.VMEM)] * (len(ordered) + len(others) + len(mines)),
        out_specs=[pl.BlockSpec(memory_space=pltpu.VMEM)] * (4 + inner),
        scratch_shapes=[
            pltpu.VMEM((spread, 2 * head), BF16),
            pltpu.VMEM((length, 2 * head), F32),
            pltpu.VMEM((capacity, 2 * head), F32),
            pltpu.VMEM((length + capacity, ROWS), F32),
            pltpu.VMEM((length + capacity, ROWS), BF16),
            pltpu.VMEM((length + capacity, ROWS), F32),
        ],
        compiler_params=pltpu.CompilerParams(vmem_limit_bytes=36 * 1024 * 1024),
        cost_estimate=pl.CostEstimate(flops=24 * capacity * length * head, bytes_accessed=16 * length * head, transcendentals=0),
        name="reply_pass",
    )(scalars, lengths, owners, *ordered, *others, *mines)


def place_kernel(inner, place_ref, *refs):
    out_ref = refs[-1]
    share = out_ref.shape[0] // (2 * inner)
    for k, ref in enumerate(refs[:-1]):
        there = lax.rem(lax.rem(place_ref[0], inner) + (inner - k), inner)
        for outer in range(2):
            at = pl.multiple_of((outer * inner + there) * share, share)
            out_ref[pl.ds(at, share), :] = ref[outer * share : (outer + 1) * share, :]


def placed_in_order(place, pieces):
    rows, width = pieces[0].shape
    return pl.pallas_call(
        functools.partial(place_kernel, len(pieces)),
        out_shape=jax.ShapeDtypeStruct((len(pieces) * rows, width), BF16),
        in_specs=[pl.BlockSpec(memory_space=pltpu.SMEM)] + [pl.BlockSpec(memory_space=pltpu.VMEM)] * len(pieces),
        out_specs=pl.BlockSpec(memory_space=pltpu.VMEM),
        compiler_params=pltpu.CompilerParams(vmem_limit_bytes=8 * 1024 * 1024),
        name="placed_in_order",
    )(place, *pieces)


def join_kernel(total_ref, arrived_ref, *refs):
    *pieces, shares_ref, part_ref = refs
    shares_ref[...] = (total_ref[...].astype(F32) + arrived_ref[...].astype(F32)).astype(BF16)
    part = pieces[0][...].astype(F32)
    for ref in pieces[1:]:
        part = part + ref[...].astype(F32)
    part_ref[...] = part.astype(BF16)


def join(total, arrived, pieces):
    return pl.pallas_call(
        join_kernel,
        out_shape=[jax.ShapeDtypeStruct(total.shape, BF16), jax.ShapeDtypeStruct(pieces[0].shape, BF16)],
        in_specs=[pl.BlockSpec(memory_space=pltpu.VMEM)] * (2 + len(pieces)),
        out_specs=[pl.BlockSpec(memory_space=pltpu.VMEM)] * 2,
        compiler_params=pltpu.CompilerParams(vmem_limit_bytes=16 * 1024 * 1024),
        name="join_sums",
    )(total, arrived, *pieces)


def per_device(
    prompt_query,
    prompt_cache,
    prompt_cotangent,
    reply_query,
    reply_cache,
    reply_cotangent,
    reply_lengths,
    reply_owner,
):
    width = prompt_cache.shape[2]
    scaling = (width // 2) ** (-0.5)
    capacity = reply_query.shape[0]
    ctx_count, comp_count, group_count = (lax.axis_size(name) for name in ("ctx", "comp", "grp"))
    inner, comp_inner = ctx_count // 2, comp_count // 2
    place = lax.axis_index("ctx").astype(jnp.int32).reshape(1)
    group = lax.axis_index("grp").astype(jnp.int32).reshape(1)

    def swap(x):
        return lax.ppermute(x, "grp", [(0, 1), (1, 0)])

    def along_z(x, k):
        pairs = [(i, i // inner * inner + (i + k) % inner) for i in range(ctx_count)]
        return lax.ppermute(x, "ctx", pairs)

    def outer_swap(x):
        return lax.ppermute(x, "ctx", [(i, (i + inner) % ctx_count) for i in range(ctx_count)])

    def along_y(x, k):
        pairs = []
        for ctx in range(ctx_count):
            for comp in range(comp_count):
                y = (2 * (comp // comp_inner) + ctx // inner + k) % 4
                to_ctx = y % 2 * inner + ctx % inner
                to_comp = y // 2 * comp_inner + comp % comp_inner
                pairs.append((ctx * comp_count + comp, to_ctx * comp_count + to_comp))
        return lax.ppermute(x, ("ctx", "comp"), pairs)

    reply_scalars = (jnp.concatenate([place, group]), reply_lengths[0], reply_owner[0])
    with jax.named_scope("order_rows"):
        ordered = order_rows(*reply_scalars, reply_query, reply_cotangent, reply_cache)
    with jax.named_scope("gather_keys"):
        own = prompt_cache[0]
        next_1, next_3 = along_z(own, 1), along_z(own, inner - 1)
        y_0 = along_y(own, 1)
        half = own.shape[0] // 2
        next_2a = along_z(stack_after(y_0, [next_1[:half]]), 1)
        next_2b = along_z(stack_after(y_0, [next_3[half:]]), inner - 1)
        y_1, y_3 = along_y(next_1, 1), along_y(next_3, -1)
        y_2a, y_2b = along_y(next_2a, 1), along_y(next_2b, -1)
        mines = [own, next_1, next_2a, next_2b, next_3, y_0, y_1, y_2a, y_2b, y_3]
        early, late = [own, next_1, next_3], [next_2a, next_2b, y_0, y_1, y_2a, y_2b, y_3]
        others = [swap(jnp.concatenate(early, axis=0)), swap(stack_after(ordered[3], late))]
        other_order = (0, 1, 3, 2, 4, 5, 6, 7)

    with jax.named_scope("reply_rows"):
        scalars, lengths, owners = reply_scalars
        reply_out, reply_dq, other_sum, mine_sum, *own_pieces = reply_pass(
            scalars, inner, lengths, owners, ordered, others, other_order, mines, scaling
        )
    arrived = swap(other_sum)
    with jax.named_scope("prompt_rows"):
        prompt_out, prompt_dq, total = prompt_pass(
            place, inner, prompt_query[0], prompt_cotangent[0], mines, mine_sum, scaling
        )

    with jax.named_scope("prompt_cache_sum"):
        count = ctx_count * comp_count
        came = [along_z(own_pieces[k], k) for k in range(1, inner)]
        shares, part = join(total, arrived, [own_pieces[0], *came])
        terms = lax.all_to_all(shares.reshape(count, -1, width), ("ctx", "comp"), 0, 0, tiled=True)
    with jax.named_scope("reply_cache_sum"):
        part = (part.astype(F32) + outer_swap(part).astype(F32)).astype(BF16)
        reply_grad = placed_in_order(place, [part] + [along_z(part, k) for k in range(1, inner)])
    with jax.named_scope("prompt_cache_halves"):
        summed = jnp.sum(terms.astype(F32), axis=0).astype(BF16)
        rows = summed.shape[0] // group_count
        first, second = summed[:rows], summed[rows:]
        is_first = group[0] == 0
        kept = jnp.where(is_first, first, second)
        came = swap(jnp.where(is_first, second, first))
        prompt_grad = jnp.where(is_first, jnp.stack([kept, came]), jnp.stack([came, kept]))
    return (
        prompt_out[None],
        prompt_dq[None],
        prompt_grad,
        reply_out,
        reply_dq,
        reply_grad,
    )


def solution(mesh):
    return jax.shard_map(
        per_device,
        mesh=mesh,
        in_specs=(
            P("grp", "ctx", "comp"),
            P("grp", "ctx", None),
            P("grp", "ctx", "comp"),
            P(("comp", "grp"), "ctx"),
            P(("comp", "grp"), None),
            P(("comp", "grp"), "ctx"),
            P(("comp", "grp"), None),
            P(("comp", "grp"), None),
        ),
        out_specs=(
            P("grp", "ctx", "comp"),
            P("grp", "ctx", "comp"),
            P(None, ("ctx", "comp", "grp"), None),
            P(("comp", "grp"), "ctx"),
            P(("comp", "grp"), "ctx"),
            P(("comp", "grp"), None),
        ),
        check_vma=False,
    )
```
